32 devices in a mesh: groups: 2 (over y), ctx: 4 (over z), head: 2 (over x), sub: 2 (over core).
Axes of the slice: x: 2, y: 2, z: 4, core: 2. Of those that a mesh axis runs over, the one named last changes fastest.
Arguments:
- inputs: bfloat16 [4096, 2048], P(('groups', 'ctx')), parts along dimension 0, may hold values from -1.5 to 1.5
- w_in: bfloat16 [2048, 4096], P(None, 'head'), may hold values from -0.125 to 0.125
- b_in: bfloat16 [4096, 128], P(('groups', 'ctx'), 'sub'), parts along dimension 0, may hold values from -6 to 6
- c_in: bfloat16 [4096, 128], P(('groups', 'ctx'), 'sub'), parts along dimension 0, may hold values from -6 to 6
- log_decay: float32 [64, 4096], P('head', ('groups', 'ctx')), parts along dimension 1, as said below
- level_weight: float32 [3, 64, 4096], P(None, 'head', ('groups', 'ctx')), parts along dimension 2, may hold values from 0.2 to 1
- out_grad: bfloat16 [4096, 4096], P(('groups', 'ctx'), 'head'), parts along dimension 0, may hold values from -0.03125 to 0.03125
Outputs:
- grad_inputs: bfloat16 [4096, 2048], P(('groups', 'ctx'), ('head', 'sub')), parts along dimension 0
- grad_b: bfloat16 [4096, 128], P(('groups', 'ctx', 'head'), 'sub'), parts along dimension 0
- grad_c: bfloat16 [4096, 128], P(('groups', 'ctx', 'head'), 'sub'), parts along dimension 0
The draws below stay inside these ranges and needn't reach their ends.
There are 2 independent parts, one for each index of `groups`. The reference program is written for one: setup_inputs(seed, part) draws one part's arguments, and reference() takes and returns one part's arrays. A program takes and returns all parts, laid end to end along the dimension named above; an argument that names none is the same for every part. Nothing has to cross between parts.
Inputs may be any that keep to these rules, and one draw needn't show every extreme that they name: `log_decay`: each entry is negative.
All inputs are finite; a program needn't handle non-finite values.
Results may differ from the reference program's by a relative error of at most 0.015.
Values may be sent and summed in bfloat16 or wider, within the bound.
A program may use at most 128 MiB of HBM per device.

```python
import math
import jax
import jax.numpy as jnp
from jax import lax

D = 2048
HEAD_COUNT = 64
HDIM = 64
STATE = 128
BLOCK_TOKENS = 512
LEVELS = 2
TOKEN_COUNT = 2048


def draw_log_decay(key, part):
    random_subkeys = jax.random.split(key, 7)
    block_list = TOKEN_COUNT // BLOCK_TOKENS
    low_log = math.log(0.005 / TOKEN_COUNT)
    head_decay_rate = jnp.exp(jax.random.uniform(random_subkeys[0], (HEAD_COUNT, 1), minval=low_log, maxval=math.log(1.0 / 30.0)))
    block_multiplier = jnp.exp(jax.random.uniform(random_subkeys[3], (HEAD_COUNT, block_list, 1), minval=math.log(0.5), maxval=math.log(2.0)))
    small_noise = jax.random.uniform(random_subkeys[4], (HEAD_COUNT, block_list, BLOCK_TOKENS), minval=0.5, maxval=1.5)
    spike_mask = jax.random.uniform(random_subkeys[5], (HEAD_COUNT, block_list, BLOCK_TOKENS)) < 3.0 / TOKEN_COUNT
    spike_depth = jax.random.uniform(random_subkeys[6], (HEAD_COUNT, block_list, BLOCK_TOKENS), minval=0.22, maxval=0.69)
    value_rows = -head_decay_rate[:, :, None] * block_multiplier * small_noise - jnp.where(spike_mask, spike_depth, 0.0)
    return value_rows.reshape(HEAD_COUNT, TOKEN_COUNT).astype(jnp.float32)


def shard_levels(key, dims, cuts, least, high):
    loudness, own = 1.0, jax.random.fold_in(key, 6)
    for axis_at, shards_of in cuts:
        draws = jnp.exp(jax.random.uniform(jax.random.fold_in(own, axis_at), (shards_of,), jnp.float32, least / len(cuts), high / len(cuts)))
        loudness = loudness * jnp.repeat(draws, dims[axis_at] // shards_of).reshape([-1 if axis == axis_at else 1 for axis in range(len(dims))])
    return loudness


def centred(stream_key, dims, scale, reach, cuts=(), kind=jnp.bfloat16):
    result = scale * jax.random.normal(stream_key, dims, jnp.float32)
    if cuts:
        result = result * shard_levels(stream_key, dims, cuts, -0.22, 0.18)
    return jnp.clip(result, -reach, reach).astype(kind)


def setup_inputs(seed: int = 0, part: int = 0) -> dict:
    seeds = jax.random.split(jax.random.key(seed), 8)
    part_splits = jax.random.split(jax.random.fold_in(seeds[7], part), 8)
    return {
        "inputs": centred(part_splits[0], (TOKEN_COUNT, D), 0.25, 1.5, ((0, 4),)),
        "w_in": centred(seeds[1], (D, HEAD_COUNT * HDIM), D ** -0.5, 0.125, ((1, 2),)),
        "b_in": centred(part_splits[2], (TOKEN_COUNT, STATE), 1.0, 6.0, ((0, 4), (1, 2))),
        "c_in": centred(part_splits[3], (TOKEN_COUNT, STATE), 1.0, 6.0, ((0, 4), (1, 2))),
        "log_decay": draw_log_decay(jax.random.fold_in(jax.random.fold_in(seeds[7], part), 71), part),
        "level_weight": jnp.clip(0.2 + 0.8 * jax.random.uniform(part_splits[5], (LEVELS + 1, HEAD_COUNT, TOKEN_COUNT), jnp.float32) ** shard_levels(part_splits[5], (LEVELS + 1, HEAD_COUNT, TOKEN_COUNT), ((1, 2), (2, 4)), -0.2, 0.2), 0.2, 1.0),
        "out_grad": centred(part_splits[6], (TOKEN_COUNT, HEAD_COUNT * HDIM), 0.005, 0.03125, ((0, 4), (1, 2))),
    }


highest = lax.Precision.HIGHEST


def shift_down(value_rows, offset):
    zero_pad = jnp.zeros((offset,) + value_rows.shape[1:], value_rows.dtype)
    return jnp.concatenate([zero_pad, value_rows[:-offset]], axis=0)


def shift_up(value_rows, offset):
    zero_pad = jnp.zeros((offset,) + value_rows.shape[1:], value_rows.dtype)
    return jnp.concatenate([value_rows[offset:], zero_pad], axis=0)


def reference(inputs, w_in, b_in, c_in, log_decay, level_weight, out_grad):
    num_shards = TOKEN_COUNT // BLOCK_TOKENS
    tok_rows = BLOCK_TOKENS
    projected = jnp.dot(inputs, w_in, preferred_element_type=jnp.float32).astype(jnp.bfloat16)
    proj_f32 = projected.astype(jnp.float32).reshape(num_shards, tok_rows, HEAD_COUNT, HDIM)
    grad_f32 = out_grad.astype(jnp.float32).reshape(num_shards, tok_rows, HEAD_COUNT, HDIM)
    b_f32 = b_in.astype(jnp.float32).reshape(num_shards, tok_rows, STATE)
    c_f32 = c_in.astype(jnp.float32).reshape(num_shards, tok_rows, STATE)
    cumulative = jnp.cumsum(log_decay.reshape(HEAD_COUNT, num_shards, tok_rows), axis=2)
    block_total = cumulative[:, :, -1]
    end_weight = jnp.exp(block_total[:, :, None] - cumulative)
    end_state = jnp.einsum('hsu,sun,suhp->shnp', end_weight, b_f32, proj_f32, precision=highest)
    window_state = end_state
    window_log = block_total.T
    gap_log = jnp.zeros_like(window_log)
    arrived_list, gap_list, window_list = [], [], []
    for level_idx in range(LEVELS):
        offset = 2 ** level_idx
        arrived = shift_down(window_state, offset)
        arrived_log = shift_down(window_log, offset)
        arrived_list.append(arrived)
        gap_list.append(gap_log)
        window_list.append(window_log)
        window_state = window_state + jnp.exp(window_log)[:, :, None, None] * arrived
        window_log = window_log + arrived_log
        gap_log = gap_log + arrived_log
    weights = level_weight.reshape(LEVELS + 1, HEAD_COUNT, num_shards, tok_rows)
    inter_c = jnp.zeros((num_shards, tok_rows, STATE), jnp.float32)
    arrived_grads = []
    for level_idx in range(LEVELS):
        level_coef = weights[level_idx + 1] * jnp.exp(cumulative + gap_list[level_idx].T[:, :, None])
        arrived_grads.append(jnp.einsum('hst,stn,sthp->shnp', level_coef, c_f32, grad_f32, precision=highest))
        inter_c = inter_c + jnp.einsum('hst,shnp,sthp->stn', level_coef, arrived_list[level_idx], grad_f32, precision=highest)
    state_grad = jnp.zeros_like(end_state)
    for level_idx in reversed(range(LEVELS)):
        returned = arrived_grads[level_idx] + jnp.exp(window_list[level_idx])[:, :, None, None] * state_grad
        state_grad = state_grad + shift_up(returned, 2 ** level_idx)
    positions = jnp.arange(tok_rows)
    causal = positions[:, None] >= positions[None, :]

    def one_block(pieces):
        b_blk, c_blk, proj_blk, grad_blk, cum_blk, lam_blk, wt_blk, sgrad_blk = pieces
        scores = jnp.einsum('tn,un->tu', c_blk, b_blk, precision=highest)
        log_gap = cum_blk[:, :, None] - cum_blk[:, None, :]
        mask_decay = jnp.where(causal, jnp.exp(jnp.where(causal, log_gap, 0.0)), 0.0)
        pair_dots = jnp.einsum('thp,uhp->htu', grad_blk, proj_blk, precision=highest)
        z_total = jnp.sum(mask_decay * lam_blk[:, :, None] * pair_dots, axis=0)
        local_weight = lax.optimization_barrier((mask_decay * scores[None] * lam_blk[:, :, None]).astype(jnp.bfloat16)).astype(jnp.float32)
        z_round = lax.optimization_barrier(z_total.astype(jnp.bfloat16)).astype(jnp.float32)
        grad_x = jnp.einsum('htu,thp->uhp', local_weight, grad_blk, precision=highest)
        grad_x = grad_x + jnp.einsum('hu,hnp,un->uhp', wt_blk, sgrad_blk, b_blk, precision=highest)
        grad_b = jnp.dot(z_round.T, c_blk, precision=highest)
        grad_b = grad_b + jnp.einsum('hu,hnp,uhp->un', wt_blk, sgrad_blk, proj_blk, precision=highest)
        grad_c = jnp.dot(z_round, b_blk, precision=highest)
        return grad_x, grad_b, grad_c

    grad_x, grad_b, grad_c = lax.map(one_block, (b_f32, c_f32, proj_f32, grad_f32, jnp.transpose(cumulative, (1, 0, 2)), jnp.transpose(weights[0], (1, 0, 2)), jnp.transpose(end_weight, (1, 0, 2)), state_grad))
    grad_c = grad_c + inter_c
    grad_x_b = grad_x.reshape(TOKEN_COUNT, HEAD_COUNT * HDIM).astype(jnp.bfloat16)
    grad_inputs = jnp.dot(grad_x_b, w_in.T, preferred_element_type=jnp.float32).astype(jnp.bfloat16)
    return grad_inputs, grad_b.reshape(TOKEN_COUNT, STATE).astype(jnp.bfloat16), grad_c.reshape(TOKEN_COUNT, STATE).astype(jnp.bfloat16)
```

```python
import functools
import jax
import jax.numpy as jnp
from jax import lax
from jax.experimental import pallas as pl
from jax.experimental.pallas import tpu as pltpu
from jax.sharding import PartitionSpec as P

F32, BF16 = jnp.float32, jnp.bfloat16
MESH = pl.DeviceIdType.MESH
CHUNK = 256


def mm(a, b):
    return lax.dot_general(a, b, (((1,), (0,)), ((), ())), preferred_element_type=F32)


def mm_nt(a, b):
    return lax.dot_general(a, b, (((1,), (1,)), ((), ())), preferred_element_type=F32)


def remote(src, dst, sems, idx, where):
    return pltpu.make_async_remote_copy(
        src_ref=src, dst_ref=dst, send_sem=sems.at[0, idx], recv_sem=sems.at[1, idx],
        device_id=where, device_id_type=MESH)


def kernel(dims, x_hbm, w_hbm, g_hbm, b_ref, c_ref, dec_ref, lw_ref,
           out_ref, gb_ref, gc_ref,
           x_v, wa_v, wb_v, g_v, b_oth, c_oth, b_v, c_v, bt_v, ct_v,
           coef_v, cumc_v, cumr_v, lam_v, wlog, alog, gap,
           gl_v, p_v, pe_v, a_v, e_v, win_s, arr_v, ret_s, came_v, sg_v,
           sc_v, scb_v, z_v, gxl_v, gx_v, part_s, part_r, own_v, gbc_s, gbc_r,
           ld_sem, bc_sem, log_sem, fwd_sem, bwd_sem, gx_sem, part_sem, gbc_sem):
    T, H, HP, HD, NS, NH, NCTX, LV, OC, RB = dims
    half, quarter = T // 2, T // 4
    hpc = CHUNK // HD
    nchunk = HP // CHUNK
    n_half = b_ref.shape[1]
    N = n_half * NS
    tok_own = T // NH
    blk = T // RB
    sub = lax.axis_index("sub")
    ctx = lax.axis_index("ctx")
    head = lax.axis_index("head")
    other = 1 - sub

    def cols(c):
        return pl.ds(pl.multiple_of(c * CHUNK, CHUNK), CHUNK)

    loads = [
        pltpu.make_async_copy(g_hbm.at[:, pl.ds(pl.multiple_of(sub * HP, 128), HP)], g_v, ld_sem.at[0]),
        pltpu.make_async_copy(x_hbm, x_v, ld_sem.at[1]),
        pltpu.make_async_copy(w_hbm.at[:, pl.ds(pl.multiple_of(sub * HP, 128), HP)], wa_v, ld_sem.at[2]),
    ]
    for k in range(NH):
        loads.append(pltpu.make_async_copy(
            w_hbm.at[pl.ds(pl.multiple_of((k * NS + sub) * OC, 128), OC), :], wb_v.at[k], ld_sem.at[3 + k]))
    for ld in loads:
        ld.start()

    barrier = pltpu.get_barrier_semaphore()
    count = NH * NS - 1
    for dh in range(NH):
        for ds in range(NS):
            if dh or ds:
                pl.semaphore_signal(barrier, inc=1, device_id={
                    "head": lax.rem(head + dh, NH), "sub": lax.rem(sub + ds, NS)}, device_id_type=MESH)
    for l in range(LV):
        hop = 2 ** l
        up, down = ctx + hop < NCTX, ctx - hop >= 0
        count = count + up.astype(jnp.int32) + down.astype(jnp.int32)

        @pl.when(up)
        def _():
            pl.semaphore_signal(barrier, inc=1, device_id={"ctx": ctx + hop}, device_id_type=MESH)

        @pl.when(down)
        def _():
            pl.semaphore_signal(barrier, inc=1, device_id={"ctx": ctx - hop}, device_id_type=MESH)
    pl.semaphore_wait(barrier, count)

    bc_copies = [remote(b_ref, b_oth, bc_sem, 0, {"sub": other}), remote(c_ref, c_oth, bc_sem, 1, {"sub": other})]
    for cp in bc_copies:
        cp.start()

    def own_rows(v):
        r = v[:H]
        for k in range(1, NS):
            r = jnp.where(sub == k, v[k * H:(k + 1) * H], r)
        return r

    rows = [own_rows(dec_ref[...])] + [own_rows(lw_ref[l]) for l in range(LV + 1)]
    used = H * len(rows)
    stacked = jnp.concatenate(rows + [jnp.zeros((128 - used, T), F32)], axis=0)
    turned = jnp.transpose(stacked)
    dec_t = turned[:, :H]
    lam_t = turned[:, H:2 * H]
    r_i = lax.broadcasted_iota(jnp.int32, (T, T), 0)
    c_i = lax.broadcasted_iota(jnp.int32, (T, T), 1)
    tri = jnp.where(r_i >= c_i, 1.0, 0.0).astype(BF16)
    d1 = dec_t.astype(BF16)
    rest = dec_t - d1.astype(F32)
    d2 = rest.astype(BF16)
    d3 = (rest - d2.astype(F32)).astype(BF16)
    cum_t = mm(tri, d1) + (mm(tri, d2) + mm(tri, d3))
    cum_r = jnp.transpose(jnp.concatenate([cum_t, jnp.zeros((T, 128 - H), F32)], axis=1))
    for c in range(nchunk):
        cumr_v[c, :hpc] = cum_r[c * hpc:(c + 1) * hpc]
        lam_v[c, :hpc] = rows[1][c * hpc:(c + 1) * hpc]
        cumc_v[c] = cum_t[:, c * hpc:(c + 1) * hpc]
    tot = cum_t[T - 1:T]
    grow = jnp.exp(cum_t)
    coef_v[0] = jnp.exp(jnp.minimum(tot - cum_t, 0.0))
    for l in range(LV):
        coef_v[1 + l] = turned[:, (l + 2) * H:(l + 3) * H] * grow
    ref_a = cum_t[half - 1:half]
    coef_v[1 + LV] = jnp.concatenate([
        jnp.exp(jnp.minimum(ref_a - cum_t[:half], 0.0)),
        lam_t[half:] * jnp.exp(jnp.minimum(cum_t[half:] - ref_a, 0.0))], axis=0)
    pieces = []
    for base in (0, half):
        mid = base + quarter
        ref_b = cum_t[mid - 1:mid]
        pieces.append(jnp.exp(jnp.minimum(ref_b - cum_t[base:mid], 0.0)))
        pieces.append(lam_t[mid:mid + quarter] * jnp.exp(jnp.minimum(cum_t[mid:mid + quarter] - ref_b, 0.0)))
    coef_v[2 + LV] = jnp.concatenate(pieces, axis=0)

    def selector(c, dtype):
        h_i = lax.broadcasted_iota(jnp.int32, (H, CHUNK), 0)
        l_i = lax.broadcasted_iota(jnp.int32, (H, CHUNK), 1)
        return jnp.where(h_i == c * hpc + lax.div(l_i, HD), 1.0, 0.0).astype(dtype)

    def spread(v, c):
        sel = selector(c, BF16)
        hi = v.astype(BF16)
        lo = (v - hi.astype(F32)).astype(BF16)
        return mm(hi, sel) + mm(lo, sel)

    tot8 = jnp.broadcast_to(tot, (8, H))
    t1 = tot8.astype(BF16)
    rest = tot8 - t1.astype(F32)
    t2 = rest.astype(BF16)
    t3 = (rest - t2.astype(F32)).astype(BF16)
    for c in range(nchunk):
        sel = selector(c, BF16)
        wlog[0, :, c * CHUNK:(c + 1) * CHUNK] = mm(t1, sel) + (mm(t2, sel) + mm(t3, sel))
    gap[0] = jnp.zeros((8, HP), F32)

    def shift(l, sign, src, dst, sems, idx):
        hop = sign * 2 ** l
        sends = (ctx + hop < NCTX) & (ctx + hop >= 0)
        gets = (ctx - hop < NCTX) & (ctx - hop >= 0)
        cp = remote(src, dst, sems, idx, {"ctx": ctx + hop})

        def start():
            pl.when(sends)(cp.start)

        def arrive():
            pl.when(gets)(cp.wait_recv)

            @pl.when(jnp.logical_not(gets))
            def _():
                dst[...] = jnp.zeros(dst.shape, dst.dtype)

        def end():
            pl.when(sends)(cp.wait_send)

        return start, arrive, end

    log_moves = [shift(l, 1, wlog.at[l], alog.at[l], log_sem, l) for l in range(LV - 1)]
    fwd = [shift(l, 1, win_s.at[l], arr_v.at[l], fwd_sem, l) for l in range(LV)]
    bwd = [shift(l, -1, ret_s.at[l], came_v.at[l], bwd_sem, l) for l in range(LV)]

    if LV > 1:
        log_moves[0][0]()

    for cp in bc_copies:
        cp.wait_recv()
    b_v[:, :n_half] = b_ref[...]
    b_v[:, n_half:] = b_oth[...]
    c_v[:, :n_half] = c_ref[...]
    c_v[:, n_half:] = c_oth[...]
    bt_v[...] = jnp.transpose(b_v[...].astype(F32)).astype(BF16)
    ct_v[...] = jnp.transpose(c_v[...].astype(F32)).astype(BF16)
    loads[0].wait()

    def level_grads(l):
        @pl.loop(0, nchunk)
        def _(c):
            gl = (g_v[:, cols(c)].astype(F32) * spread(coef_v[1 + l], c)).astype(BF16)
            gl_v[l, :, cols(c)] = gl
            a_v[l, :, cols(c)] = mm(ct_v[...], gl)

    level_grads(LV - 1)
    for l in range(LV - 1):
        log_moves[l][1]()
        gap[l + 1] = gap[l] + alog[l]
        wlog[l + 1] = wlog[l] + alog[l]
        if l + 1 < LV - 1:
            log_moves[l + 1][0]()
    ret_s[LV - 1] = (a_v[LV - 1] * jnp.exp(gap[LV - 1, 0:1])).astype(BF16)
    bwd[LV - 1][0]()

    loads[1].wait()
    loads[2].wait()

    @pl.loop(0, nchunk)
    def _(c):
        proj = mm(x_v[...], wa_v[:, cols(c)]).astype(BF16)
        p_v[:, cols(c)] = proj
        pe = (proj.astype(F32) * spread(coef_v[0], c)).astype(BF16)
        pe_v[:, cols(c)] = pe
        e = mm(bt_v[...], pe)
        e_v[:, cols(c)] = e
        win_s[0, :, cols(c)] = e.astype(BF16)

    fwd[0][0]()
    for l in range(LV - 1):
        level_grads(l)

    sc_v[...] = mm_nt(b_v[...], c_v[...])
    scb_v[...] = sc_v[...].astype(BF16)
    z_v[...] = jnp.zeros((T, T), F32)

    def off_block(c, coef, u0, t0, size):
        us, ts = slice(u0, u0 + size), slice(t0, t0 + size)
        eb = spread(coef_v[coef, us], c)
        ga = (g_v[ts, cols(c)].astype(F32) * spread(coef_v[coef, ts], c)).astype(BF16)
        pb = (p_v[us, cols(c)].astype(F32) * eb).astype(BF16)
        z_v[us, ts] += mm_nt(pb, ga)
        return eb * mm(scb_v[us, ts], ga)

    @pl.loop(0, nchunk)
    def _(c):
        far = off_block(c, 1 + LV, 0, half, half)
        near_a = off_block(c, 2 + LV, 0, quarter, quarter)
        near_b = off_block(c, 2 + LV, half, half + quarter, quarter)
        gxl_v[:half, cols(c)] = far
        gxl_v[:quarter, cols(c)] += near_a
        gxl_v[half:half + quarter, cols(c)] = near_b
        gxl_v[quarter * 3:, cols(c)] = jnp.zeros((quarter, CHUNK), F32)

    state = [None]

    def ladder(l):
        fwd[l][1]()
        keep = e_v[...] if l == 0 else e_v[...]
        e_v[...] = keep + jnp.exp(wlog[l, 0:1]) * arr_v[l].astype(F32)
        win_s[l + 1] = e_v[...].astype(BF16)
        fwd[l + 1][0]()
        k = LV - 1 - l
        bwd[k][1]()
        if l == 0:
            sg_v[...] = came_v[k].astype(F32)
        else:
            sg_v[...] += came_v[k].astype(F32)
        ret_s[k - 1] = (a_v[k - 1] * jnp.exp(gap[k - 1, 0:1])
                        + jnp.exp(wlog[k - 1, 0:1]) * sg_v[...]).astype(BF16)
        bwd[k - 1][0]()

    for l in range(LV - 1):
        ladder(l)

    q_r = lax.broadcasted_iota(jnp.int32, (quarter, quarter), 0)
    q_c = lax.broadcasted_iota(jnp.int32, (quarter, quarter), 1)

    @pl.loop(0, nchunk)
    def _(c):
        keep = q_c >= q_r
        for i in range(4):
            sl = slice(i * quarter, (i + 1) * quarter)
            p_b, g_b = p_v[sl, cols(c)], g_v[sl, cols(c)]
            zsum = z_v[sl, sl]
            locals_x = []
            for j in range(hpc):
                lanes = slice(j * HD, (j + 1) * HD)
                row = cumr_v[c, j:j + 1, sl]
                lam = lam_v[c, j:j + 1, sl]
                col = cumc_v[c, sl, j:j + 1]
                dec = jnp.where(keep, jnp.exp(jnp.minimum(row - col, 0.0)) * lam, 0.0)
                zsum = zsum + dec * mm_nt(p_b[:, lanes], g_b[:, lanes])
                lwt = (dec * sc_v[sl, sl]).astype(BF16)
                locals_x.append(mm(lwt, g_b[:, lanes]))
            z_v[sl, sl] = zsum
            gxl_v[sl, cols(c)] += jnp.concatenate(locals_x, axis=1)

    bwd[0][1]()
    if LV > 1:
        sg_v[...] += came_v[0].astype(F32)
    else:
        sg_v[...] = came_v[0].astype(F32)
    sgb = sg_v[...].astype(BF16)
    came_v[0] = sgb
    gx_copies = []
    for r in range(RB):
        rs = slice(r * blk, (r + 1) * blk)

        @pl.loop(0, nchunk)
        def _(c):
            ew = spread(coef_v[0, rs], c)
            gx = gxl_v[rs, cols(c)] + ew * mm(b_v[rs], came_v[0, :, cols(c)])
            gx_v[sub, rs, cols(c)] = gx.astype(BF16)

        cp = remote(gx_v.at[sub, pl.ds(r * blk, blk)], gx_v.at[sub, pl.ds(r * blk, blk)], gx_sem, r, {"sub": other})
        cp.start()
        gx_copies.append(cp)

    for k in range(NH):
        loads[3 + k].wait()
    part_copies = []
    for r in range(RB):
        rs = slice(r * blk, (r + 1) * blk)
        gx_copies[r].wait_recv()
        for d in range(1, NH):
            k = lax.rem(head + d, NH)

            part = mm_nt(gx_v[0, rs], wb_v[k, :, :HP]) + mm_nt(gx_v[1, rs], wb_v[k, :, HP:])
            part_s[d - 1, rs] = part.astype(BF16)
            cp = remote(part_s.at[d - 1, pl.ds(r * blk, blk)], part_r.at[d - 1, pl.ds(r * blk, blk)],
                        part_sem, (d - 1) * RB + r, {"head": k})
            cp.start()
            part_copies.append(cp)

    fwd[LV - 1][1]()
    gb_all = mm(z_v[...].astype(BF16), c_v[...]) + mm_nt(pe_v[...], came_v[0])
    gc_all = mm(jnp.transpose(z_v[...]).astype(BF16), b_v[...])
    for l in range(LV):
        gc_all = gc_all + mm_nt(gl_v[l], (arr_v[l].astype(F32) * jnp.exp(gap[l, 0:1])).astype(BF16))
    gbc_copies = []
    gbc_s[0, 0] = gb_all[:, :n_half].astype(BF16)
    gbc_s[0, 1] = gc_all[:, :n_half].astype(BF16)
    gbc_s[1, 0] = gb_all[:, n_half:].astype(BF16)
    gbc_s[1, 1] = gc_all[:, n_half:].astype(BF16)
    for dh in range(NH):
        for ds in range(NS):
            if dh or ds:
                k = lax.rem(head + dh, NH)
                n = dh * NS + ds - 1
                cp = remote(gbc_s.at[ds, :, pl.ds(pl.multiple_of(k * tok_own, 16), tok_own)], gbc_r.at[n],
                            gbc_sem, n, {"head": k, "sub": lax.rem(sub + ds, NS)})
                cp.start()
                gbc_copies.append(cp)
    for r in range(RB):
        rs = slice(r * blk, (r + 1) * blk)
        own_v[rs] = mm_nt(gx_v[0, rs], wb_v[head, :, :HP]) + mm_nt(gx_v[1, rs], wb_v[head, :, HP:])
    own_tok = pl.ds(pl.multiple_of(head * tok_own, 16), tok_own)
    gb = gbc_s[0, 0, own_tok].astype(F32)
    gc = gbc_s[0, 1, own_tok].astype(F32)
    for n, cp in enumerate(gbc_copies):
        cp.wait_recv()
        gb = gb + gbc_r[n, 0].astype(F32)
        gc = gc + gbc_r[n, 1].astype(F32)
    gb_ref[...] = gb.astype(BF16)
    gc_ref[...] = gc.astype(BF16)
    for r in range(RB):
        rs = slice(r * blk, (r + 1) * blk)
        acc = own_v[rs]
        for d in range(1, NH):
            part_copies[r * (NH - 1) + d - 1].wait_recv()
            acc = acc + part_r[d - 1, rs].astype(F32)
        out_ref[rs] = acc.astype(BF16)

    for cp in bc_copies + gx_copies + part_copies + gbc_copies:
        cp.wait_send()
    for mv in log_moves + fwd + bwd:
        mv[2]()


def shards(inputs, w_in, b_in, c_in, log_decay, level_weight, out_grad):
    T, D = inputs.shape
    HG, inner = log_decay.shape[0], w_in.shape[1]
    HD = inner // HG
    NS, NH, NCTX = (lax.axis_size(a) for a in ("sub", "head", "ctx"))
    LV = level_weight.shape[0] - 1
    H = HG // NS
    HP = H * HD
    nh = b_in.shape[1]
    N = nh * NS
    OC = D // NH // NS
    RB = 4
    nchunk = HP // CHUNK
    tok_own = T // NH
    dims = (T, H, HP, HD, NS, NH, NCTX, LV, OC, RB)
    V = pltpu.VMEM
    scratch = [
        V((T, D), BF16), V((D, HP), BF16), V((NH, OC, inner), BF16), V((T, HP), BF16),
        V((T, nh), BF16), V((T, nh), BF16), V((T, N), BF16), V((T, N), BF16), V((N, T), BF16), V((N, T), BF16),
        V((LV + 3, T, H), F32), V((nchunk, T, CHUNK // HD), F32), V((nchunk, 8, T), F32), V((nchunk, 8, T), F32),
        V((LV, 8, HP), F32), V((LV, 8, HP), F32), V((LV, 8, HP), F32),
        V((LV, T, HP), BF16), V((T, HP), BF16), V((T, HP), BF16), V((LV, N, HP), F32), V((N, HP), F32),
        V((LV, N, HP), BF16), V((LV, N, HP), BF16), V((LV, N, HP), BF16), V((LV, N, HP), BF16), V((N, HP), F32),
        V((T, T), F32), V((T, T), BF16), V((T, T), F32), V((T, HP), F32), V((NS, T, HP), BF16),
        V((NH - 1, T, OC), BF16), V((NH - 1, T, OC), BF16), V((T, OC), F32),
        V((NS, 2, T, nh), BF16), V((NH * NS - 1, 2, tok_own, nh), BF16),
    ]
    S = pltpu.SemaphoreType.DMA
    scratch += [S((3 + NH,)), S((2, 2)), S((2, LV)), S((2, LV)), S((2, LV)), S((2, RB)),
                S((2, (NH - 1) * RB)), S((2, NH * NS - 1))]
    vm = pl.BlockSpec(memory_space=pltpu.VMEM)
    hb = pl.BlockSpec(memory_space=pl.ANY)
    return pl.pallas_call(
        functools.partial(kernel, dims),
        out_shape=(jax.ShapeDtypeStruct((T, OC), BF16), jax.ShapeDtypeStruct((tok_own, nh), BF16),
                   jax.ShapeDtypeStruct((tok_own, nh), BF16)),
        in_specs=[hb, hb, hb, vm, vm, vm, vm],
        out_specs=(vm, vm, vm),
        scratch_shapes=scratch,
        compiler_params=pltpu.CompilerParams(
            collective_id=0, has_side_effects=True, vmem_limit_bytes=56 * 2 ** 20),
    )(inputs, w_in, out_grad, b_in, c_in, log_decay, level_weight)


def solution(mesh):
    in_specs = (
        P(("groups", "ctx"), None),
        P(None, "head"),
        P(("groups", "ctx"), "sub"),
        P(("groups", "ctx"), "sub"),
        P("head", ("groups", "ctx")),
        P(None, "head", ("groups", "ctx")),
        P(("groups", "ctx"), "head"),
    )
    out_specs = (
        P(("groups", "ctx"), ("head", "sub")),
        P(("groups", "ctx", "head"), "sub"),
        P(("groups", "ctx", "head"), "sub"),
    )
    return jax.shard_map(shards, mesh=mesh, in_specs=in_specs, out_specs=out_specs, check_vma=False)
```

```python
import functools
import jax
import jax.numpy as jnp
from jax import lax
from jax.experimental import pallas as pl
from jax.experimental.pallas import tpu as pltpu
from jax.sharding import PartitionSpec as P

F32, BF16 = jnp.float32, jnp.bfloat16
MESH = pl.DeviceIdType.MESH
CHUNK = 256


def mm(a, b):
    return lax.dot_general(a, b, (((1,), (0,)), ((), ())), preferred_element_type=F32)


def mm_nt(a, b):
    return lax.dot_general(a, b, (((1,), (1,)), ((), ())), preferred_element_type=F32)


def remote(src, dst, sems, idx, where):
    return pltpu.make_async_remote_copy(
        src_ref=src, dst_ref=dst, send_sem=sems.at[0, idx], recv_sem=sems.at[1, idx],
        device_id=where, device_id_type=MESH)


def kernel(dims, x_hbm, w_hbm, g_hbm, b_ref, c_ref, dec_ref, lw_ref,
           out_ref, gb_ref, gc_ref,
           x_v, wa_v, wb_v, g_v, b_oth, c_oth, b_v, c_v, bt_v, ct_v,
           coef_v, cumc_v, cumr_v, lam_v, wlog, alog, gap,
           gl_v, p_v, pe_v, a_v, e_v, win_s, arr_v, ret_s, came_v, sg_v,
           sc_v, scb_v, z_v, gxl_v, gx_v, part_s, part_r, own_v, gbc_s, gbc_r,
           ld_sem, bc_sem, log_sem, fwd_sem, bwd_sem, gx_sem, part_sem, gbc_sem):
    T, H, HP, HD, NS, NH, NCTX, LV, OC, RB = dims
    half, quarter = T // 2, T // 4
    hpc = CHUNK // HD
    nchunk = HP // CHUNK
    n_half = b_ref.shape[0]
    N = n_half * NS
    tok_own = T // NH
    blk = T // RB
    sub = lax.axis_index("sub")
    ctx = lax.axis_index("ctx")
    head = lax.axis_index("head")
    other = 1 - sub

    def cols(c):
        return pl.ds(pl.multiple_of(c * CHUNK, CHUNK), CHUNK)

    loads = [
        pltpu.make_async_copy(g_hbm.at[:, pl.ds(pl.multiple_of(sub * HP, 128), HP)], g_v, ld_sem.at[0]),
        pltpu.make_async_copy(x_hbm, x_v, ld_sem.at[1]),
        pltpu.make_async_copy(w_hbm.at[:, pl.ds(pl.multiple_of(sub * HP, 128), HP)], wa_v, ld_sem.at[2]),
    ]
    for k in range(NH):
        loads.append(pltpu.make_async_copy(
            w_hbm.at[pl.ds(pl.multiple_of((k * NS + sub) * OC, 128), OC), :], wb_v.at[k], ld_sem.at[3 + k]))
    for ld in loads:
        ld.start()

    barrier = pltpu.get_barrier_semaphore()
    count = NH * NS - 1
    for dh in range(NH):
        for ds in range(NS):
            if dh or ds:
                pl.semaphore_signal(barrier, inc=1, device_id={
                    "head": lax.rem(head + dh, NH), "sub": lax.rem(sub + ds, NS)}, device_id_type=MESH)
    for l in range(LV):
        hop = 2 ** l
        up, down = ctx + hop < NCTX, ctx - hop >= 0
        count = count + up.astype(jnp.int32) + down.astype(jnp.int32)

        @pl.when(up)
        def _():
            pl.semaphore_signal(barrier, inc=1, device_id={"ctx": ctx + hop}, device_id_type=MESH)

        @pl.when(down)
        def _():
            pl.semaphore_signal(barrier, inc=1, device_id={"ctx": ctx - hop}, device_id_type=MESH)
    pl.semaphore_wait(barrier, count)

    bc_copies = [remote(b_ref, b_oth, bc_sem, 0, {"sub": other}), remote(c_ref, c_oth, bc_sem, 1, {"sub": other})]
    for cp in bc_copies:
        cp.start()

    def own_rows(v):
        r = v[:H]
        for k in range(1, NS):
            r = jnp.where(sub == k, v[k * H:(k + 1) * H], r)
        return r

    rows = [own_rows(dec_ref[...])] + [own_rows(lw_ref[l]) for l in range(LV + 1)]
    used = H * len(rows)
    stacked = jnp.concatenate(rows + [jnp.zeros((128 - used, T), F32)], axis=0)
    turned = jnp.transpose(stacked)
    dec_t = turned[:, :H]
    lam_t = turned[:, H:2 * H]
    r_i = lax.broadcasted_iota(jnp.int32, (T, T), 0)
    c_i = lax.broadcasted_iota(jnp.int32, (T, T), 1)
    tri = jnp.where(r_i >= c_i, 1.0, 0.0).astype(BF16)
    d1 = dec_t.astype(BF16)
    rest = dec_t - d1.astype(F32)
    d2 = rest.astype(BF16)
    d3 = (rest - d2.astype(F32)).astype(BF16)
    def halves(v):
        hi = v.astype(BF16)
        return jnp.concatenate([hi.astype(F32), v - hi.astype(F32)], axis=1).astype(BF16)

    cum_t = mm(tri, d1) + (mm(tri, d2) + mm(tri, d3))
    cum_r = jnp.transpose(jnp.concatenate([cum_t, jnp.zeros((T, 128 - H), F32)], axis=1))
    for c in range(nchunk):
        cumr_v[c, :hpc] = cum_r[c * hpc:(c + 1) * hpc]
        lam_v[c, :hpc] = rows[1][c * hpc:(c + 1) * hpc]
        cumc_v[c] = cum_t[:, c * hpc:(c + 1) * hpc]
    tot = cum_t[T - 1:T]
    grow = jnp.exp(cum_t)
    coef_v[0] = halves(jnp.exp(jnp.minimum(tot - cum_t, 0.0)))
    for l in range(LV):
        coef_v[1 + l] = halves(turned[:, (l + 2) * H:(l + 3) * H] * grow)
    ref_a = cum_t[half - 1:half]
    coef_v[1 + LV] = halves(jnp.concatenate([
        jnp.exp(jnp.minimum(ref_a - cum_t[:half], 0.0)),
        lam_t[half:] * jnp.exp(jnp.minimum(cum_t[half:] - ref_a, 0.0))], axis=0))
    pieces = []
    for base in (0, half):
        mid = base + quarter
        ref_b = cum_t[mid - 1:mid]
        pieces.append(jnp.exp(jnp.minimum(ref_b - cum_t[base:mid], 0.0)))
        pieces.append(lam_t[mid:mid + quarter] * jnp.exp(jnp.minimum(cum_t[mid:mid + quarter] - ref_b, 0.0)))
    coef_v[2 + LV] = halves(jnp.concatenate(pieces, axis=0))

    def selector(c, dtype):
        h_i = lax.broadcasted_iota(jnp.int32, (H, CHUNK), 0)
        l_i = lax.broadcasted_iota(jnp.int32, (H, CHUNK), 1)
        return jnp.where(h_i == c * hpc + lax.div(l_i, HD), 1.0, 0.0).astype(dtype)

    def spread(v, c):
        h_i = lax.rem(lax.broadcasted_iota(jnp.int32, (2 * H, CHUNK), 0), H)
        l_i = lax.broadcasted_iota(jnp.int32, (2 * H, CHUNK), 1)
        return mm(v, jnp.where(h_i == c * hpc + lax.div(l_i, HD), 1.0, 0.0).astype(BF16))

    tot8 = jnp.broadcast_to(tot, (8, H))
    t1 = tot8.astype(BF16)
    rest = tot8 - t1.astype(F32)
    t2 = rest.astype(BF16)
    t3 = (rest - t2.astype(F32)).astype(BF16)
    for c in range(nchunk):
        sel = selector(c, BF16)
        wlog[0, :, c * CHUNK:(c + 1) * CHUNK] = mm(t1, sel) + (mm(t2, sel) + mm(t3, sel))
    gap[0] = jnp.zeros((8, HP), F32)

    def shift(l, sign, src, dst, sems, idx):
        hop = sign * 2 ** l
        sends = (ctx + hop < NCTX) & (ctx + hop >= 0)
        gets = (ctx - hop < NCTX) & (ctx - hop >= 0)
        cp = remote(src, dst, sems, idx, {"ctx": ctx + hop})

        def start():
            pl.when(sends)(cp.start)

        def arrive():
            pl.when(gets)(cp.wait_recv)

            @pl.when(jnp.logical_not(gets))
            def _():
                dst[...] = jnp.zeros(dst.shape, dst.dtype)

        def end():
            pl.when(sends)(cp.wait_send)

        return start, arrive, end

    log_moves = [shift(l, 1, wlog.at[l], alog.at[l], log_sem, l) for l in range(LV - 1)]
    fwd = [shift(l, 1, win_s.at[l], arr_v.at[l], fwd_sem, l) for l in range(LV)]
    bwd = [shift(l, -1, ret_s.at[l], came_v.at[l], bwd_sem, l) for l in range(LV)]

    if LV > 1:
        log_moves[0][0]()

    for cp in bc_copies:
        cp.wait_recv()
    bt_v[:n_half] = b_ref[...]
    bt_v[n_half:] = b_oth[...]
    ct_v[:n_half] = c_ref[...]
    ct_v[n_half:] = c_oth[...]
    b_v[...] = jnp.transpose(bt_v[...].astype(F32)).astype(BF16)
    c_v[...] = jnp.transpose(ct_v[...].astype(F32)).astype(BF16)
    loads[0].wait()

    def level_grads(l):
        @pl.loop(0, nchunk)
        def _(c):
            gl = (g_v[:, cols(c)].astype(F32) * spread(coef_v[1 + l], c)).astype(BF16)
            gl_v[l, :, cols(c)] = gl
            a_v[l, :, cols(c)] = mm(ct_v[...], gl)

    level_grads(LV - 1)
    for l in range(LV - 1):
        log_moves[l][1]()
        gap[l + 1] = gap[l] + alog[l]
        wlog[l + 1] = wlog[l] + alog[l]
        if l + 1 < LV - 1:
            log_moves[l + 1][0]()
    ret_s[LV - 1] = (a_v[LV - 1] * jnp.exp(gap[LV - 1, 0:1])).astype(BF16)
    bwd[LV - 1][0]()

    loads[1].wait()
    loads[2].wait()

    @pl.loop(0, nchunk)
    def _(c):
        proj = mm(x_v[...], wa_v[:, cols(c)]).astype(BF16)
        p_v[:, cols(c)] = proj
        pe = (proj.astype(F32) * spread(coef_v[0], c)).astype(BF16)
        pe_v[:, cols(c)] = pe
        e = mm(bt_v[...], pe)
        e_v[:, cols(c)] = e
        win_s[0, :, cols(c)] = e.astype(BF16)

    fwd[0][0]()
    for l in range(LV - 1):
        level_grads(l)

    sc_v[...] = mm_nt(b_v[...], c_v[...])
    scb_v[...] = sc_v[...].astype(BF16)
    z_v[...] = jnp.zeros((T, T), F32)

    def off_block(c, coef, u0, t0, size):
        us, ts = slice(u0, u0 + size), slice(t0, t0 + size)
        eb = spread(coef_v[coef, us], c)
        ga = (g_v[ts, cols(c)].astype(F32) * spread(coef_v[coef, ts], c)).astype(BF16)
        pb = (p_v[us, cols(c)].astype(F32) * eb).astype(BF16)
        z_v[us, ts] += mm_nt(pb, ga)
        return eb * mm(scb_v[us, ts], ga)

    @pl.loop(0, nchunk)
    def _(c):
        far = off_block(c, 1 + LV, 0, half, half)
        near_a = off_block(c, 2 + LV, 0, quarter, quarter)
        near_b = off_block(c, 2 + LV, half, half + quarter, quarter)
        gxl_v[:half, cols(c)] = far
        gxl_v[:quarter, cols(c)] += near_a
        gxl_v[half:half + quarter, cols(c)] = near_b
        gxl_v[quarter * 3:, cols(c)] = jnp.zeros((quarter, CHUNK), F32)

    state = [None]

    def ladder(l):
        fwd[l][1]()
        keep = e_v[...] if l == 0 else e_v[...]
        e_v[...] = keep + jnp.exp(wlog[l, 0:1]) * arr_v[l].astype(F32)
        win_s[l + 1] = e_v[...].astype(BF16)
        fwd[l + 1][0]()
        k = LV - 1 - l
        bwd[k][1]()
        if l == 0:
            sg_v[...] = came_v[k].astype(F32)
        else:
            sg_v[...] += came_v[k].astype(F32)
        ret_s[k - 1] = (a_v[k - 1] * jnp.exp(gap[k - 1, 0:1])
                        + jnp.exp(wlog[k - 1, 0:1]) * sg_v[...]).astype(BF16)
        bwd[k - 1][0]()

    for l in range(LV - 1):
        ladder(l)

    q_r = lax.broadcasted_iota(jnp.int32, (quarter, quarter), 0)
    q_c = lax.broadcasted_iota(jnp.int32, (quarter, quarter), 1)

    m_c = lax.div(lax.broadcasted_iota(jnp.int32, (quarter, CHUNK), 1), HD)
    masks = [jnp.where(m_c == j, 1.0, 0.0).astype(BF16) for j in range(hpc)]

    @pl.loop(0, nchunk)
    def _(c):
        keep = q_c >= q_r
        for i in range(4):
            sl = slice(i * quarter, (i + 1) * quarter)
            p_b, g_b = p_v[sl, cols(c)], g_v[sl, cols(c)]
            dots = mm_nt(jnp.concatenate([p_b * m for m in masks], axis=0), g_b)
            zsum = z_v[sl, sl]
            weights = []
            for j in range(hpc):
                row = cumr_v[c, j:j + 1, sl]
                lam = lam_v[c, j:j + 1, sl]
                col = cumc_v[c, sl, j:j + 1]
                dec = jnp.where(keep, jnp.exp(row - col) * lam, 0.0)
                zsum = zsum + dec * dots[j * quarter:(j + 1) * quarter]
                weights.append((dec * sc_v[sl, sl]).astype(BF16))
            z_v[sl, sl] = zsum
            gxl_v[sl, cols(c)] += mm(jnp.concatenate(weights, axis=1),
                                     jnp.concatenate([g_b * m for m in masks], axis=0))

    bwd[0][1]()
    if LV > 1:
        sg_v[...] += came_v[0].astype(F32)
    else:
        sg_v[...] = came_v[0].astype(F32)
    sgb = sg_v[...].astype(BF16)
    came_v[0] = sgb
    gx_copies = []
    for r in range(RB):
        rs = slice(r * blk, (r + 1) * blk)

        @pl.loop(0, nchunk)
        def _(c):
            ew = spread(coef_v[0, rs], c)
            gx = gxl_v[rs, cols(c)] + ew * mm(b_v[rs], came_v[0, :, cols(c)])
            gx_v[sub, rs, cols(c)] = gx.astype(BF16)

        cp = remote(gx_v.at[sub, pl.ds(r * blk, blk)], gx_v.at[sub, pl.ds(r * blk, blk)], gx_sem, r, {"sub": other})
        cp.start()
        gx_copies.append(cp)

    for k in range(NH):
        loads[3 + k].wait()
    part_copies = []
    for r in range(RB):
        rs = slice(r * blk, (r + 1) * blk)
        gx_copies[r].wait_recv()
        for d in range(1, NH):
            k = lax.rem(head + d, NH)

            part = mm_nt(gx_v[0, rs], wb_v[k, :, :HP]) + mm_nt(gx_v[1, rs], wb_v[k, :, HP:])
            part_s[d - 1, rs] = part.astype(BF16)
            cp = remote(part_s.at[d - 1, pl.ds(r * blk, blk)], part_r.at[d - 1, pl.ds(r * blk, blk)],
                        part_sem, (d - 1) * RB + r, {"head": k})
            cp.start()
            part_copies.append(cp)

    fwd[LV - 1][1]()
    gb_all = mm(z_v[...].astype(BF16), c_v[...]) + mm_nt(pe_v[...], came_v[0])
    gc_all = mm(jnp.transpose(z_v[...]).astype(BF16), b_v[...])
    for l in range(LV):
        gc_all = gc_all + mm_nt(gl_v[l], (arr_v[l].astype(F32) * jnp.exp(gap[l, 0:1])).astype(BF16))
    gbc_copies = []
    gbc_s[0, 0] = gb_all[:, :n_half].astype(BF16)
    gbc_s[0, 1] = gc_all[:, :n_half].astype(BF16)
    gbc_s[1, 0] = gb_all[:, n_half:].astype(BF16)
    gbc_s[1, 1] = gc_all[:, n_half:].astype(BF16)
    for dh in range(NH):
        for ds in range(NS):
            if dh or ds:
                k = lax.rem(head + dh, NH)
                n = dh * NS + ds - 1
                cp = remote(gbc_s.at[ds, :, pl.ds(pl.multiple_of(k * tok_own, 16), tok_own)], gbc_r.at[n],
                            gbc_sem, n, {"head": k, "sub": lax.rem(sub + ds, NS)})
                cp.start()
                gbc_copies.append(cp)
    own_v[...] = mm_nt(gx_v[0], wb_v[head, :, :HP]) + mm_nt(gx_v[1], wb_v[head, :, HP:])
    own_tok = pl.ds(pl.multiple_of(head * tok_own, 16), tok_own)
    gb = gbc_s[0, 0, own_tok].astype(F32)
    gc = gbc_s[0, 1, own_tok].astype(F32)
    for n, cp in enumerate(gbc_copies):
        cp.wait_recv()
        gb = gb + gbc_r[n, 0].astype(F32)
        gc = gc + gbc_r[n, 1].astype(F32)
    both = jnp.transpose(jnp.concatenate([gb, gc], axis=1))
    gb_ref[...] = both[:n_half].astype(BF16)
    gc_ref[...] = both[n_half:].astype(BF16)
    for r in range(RB):
        rs = slice(r * blk, (r + 1) * blk)
        acc = own_v[rs]
        for d in range(1, NH):
            part_copies[r * (NH - 1) + d - 1].wait_recv()
            acc = acc + part_r[d - 1, rs].astype(F32)
        out_ref[rs] = acc.astype(BF16)

    for cp in bc_copies + gx_copies + part_copies + gbc_copies:
        cp.wait_send()
    for mv in log_moves + fwd + bwd:
        mv[2]()


def shards(inputs, w_in, b_in, c_in, log_decay, level_weight, out_grad):
    T, D = inputs.shape
    HG, inner = log_decay.shape[0], w_in.shape[1]
    HD = inner // HG
    NS, NH, NCTX = (lax.axis_size(a) for a in ("sub", "head", "ctx"))
    LV = level_weight.shape[0] - 1
    H = HG // NS
    HP = H * HD
    nh = b_in.shape[1]
    N = nh * NS
    OC = D // NH // NS
    RB = 2
    nchunk = HP // CHUNK
    tok_own = T // NH
    dims = (T, H, HP, HD, NS, NH, NCTX, LV, OC, RB)
    V = pltpu.VMEM
    scratch = [
        V((T, D), BF16), V((D, HP), BF16), V((NH, OC, inner), BF16), V((T, HP), BF16),
        V((nh, T), BF16), V((nh, T), BF16), V((T, N), BF16), V((T, N), BF16), V((N, T), BF16), V((N, T), BF16),
        V((LV + 3, T, 2 * H), BF16), V((nchunk, T, CHUNK // HD), F32), V((nchunk, 8, T), F32), V((nchunk, 8, T), F32),
        V((LV, 8, HP), F32), V((LV, 8, HP), F32), V((LV, 8, HP), F32),
        V((LV, T, HP), BF16), V((T, HP), BF16), V((T, HP), BF16), V((LV, N, HP), F32), V((N, HP), F32),
        V((LV, N, HP), BF16), V((LV, N, HP), BF16), V((LV, N, HP), BF16), V((LV, N, HP), BF16), V((N, HP), F32),
        V((T, T), F32), V((T, T), BF16), V((T, T), F32), V((T, HP), F32), V((NS, T, HP), BF16),
        V((NH - 1, T, OC), BF16), V((NH - 1, T, OC), BF16), V((T, OC), F32),
        V((NS, 2, T, nh), BF16), V((NH * NS - 1, 2, tok_own, nh), BF16),
    ]
    S = pltpu.SemaphoreType.DMA
    scratch += [S((3 + NH,)), S((2, 2)), S((2, LV)), S((2, LV)), S((2, LV)), S((2, RB)),
                S((2, (NH - 1) * RB)), S((2, NH * NS - 1))]
    vm = pl.BlockSpec(memory_space=pltpu.VMEM)
    hb = pl.BlockSpec(memory_space=pl.ANY)
    grad_inputs, grad_b, grad_c = pl.pallas_call(
        functools.partial(kernel, dims),
        out_shape=(jax.ShapeDtypeStruct((T, OC), BF16), jax.ShapeDtypeStruct((nh, tok_own), BF16),
                   jax.ShapeDtypeStruct((nh, tok_own), BF16)),
        in_specs=[hb, hb, hb, vm, vm, vm, vm],
        out_specs=(vm, vm, vm),
        scratch_shapes=scratch,
        compiler_params=pltpu.CompilerParams(
            collective_id=0, has_side_effects=True, vmem_limit_bytes=56 * 2 ** 20),
    )(inputs, w_in, out_grad, b_in.T, c_in.T, log_decay, level_weight)
    return grad_inputs, grad_b.T, grad_c.T


def solution(mesh):
    in_specs = (
        P(("groups", "ctx"), None),
        P(None, "head"),
        P(("groups", "ctx"), "sub"),
        P(("groups", "ctx"), "sub"),
        P("head", ("groups", "ctx")),
        P(None, "head", ("groups", "ctx")),
        P(("groups", "ctx"), "head"),
    )
    out_specs = (
        P(("groups", "ctx"), ("head", "sub")),
        P(("groups", "ctx", "head"), "sub"),
        P(("groups", "ctx", "head"), "sub"),
    )
    return jax.shard_map(shards, mesh=mesh, in_specs=in_specs, out_specs=out_specs, check_vma=False)
```

```python
import functools
import jax
import jax.numpy as jnp
from jax import lax
from jax.experimental import pallas as pl
from jax.experimental.pallas import tpu as pltpu
from jax.sharding import PartitionSpec as P

F32, BF16 = jnp.float32, jnp.bfloat16
MESH = pl.DeviceIdType.MESH
CHUNK = 256


def mm(a, b):
    return lax.dot_general(a, b, (((1,), (0,)), ((), ())), preferred_element_type=F32)


def mm_nt(a, b):
    return lax.dot_general(a, b, (((1,), (1,)), ((), ())), preferred_element_type=F32)


def remote(src, dst, sems, idx, where):
    return pltpu.make_async_remote_copy(
        src_ref=src, dst_ref=dst, send_sem=sems.at[0, idx], recv_sem=sems.at[1, idx],
        device_id=where, device_id_type=MESH)


def kernel(dims, x_hbm, w_hbm, g_hbm, b_ref, c_ref, dec_ref, lw_ref,
           out_ref, gb_ref, gc_ref,
           x_v, wa_v, wb_v, g_v, b_oth, c_oth, b_v, c_v, bt_v, ct_v,
           coef_v, cumc_v, cumr_v, lam_v, wlog, alog, gap,
           gl_v, p_v, pe_v, a_v, e_v, win_s, arr_v, ret_s, came_v, sg_v,
           sc_v, scb_v, z_v, gxl_v, gx_v, part_s, part_r, own_v, gbc_s, gbc_r,
           ld_sem, bc_sem, log_sem, fwd_sem, bwd_sem, gx_sem, part_sem, gbc_sem):
    T, H, HP, HD, NS, NH, NCTX, LV, OC, RB = dims
    half, quarter = T // 2, T // 4
    hpc = CHUNK // HD
    nchunk = HP // CHUNK
    n_half = b_ref.shape[0]
    N = n_half * NS
    tok_own = T // NH
    blk = T // RB
    sub = lax.axis_index("sub")
    ctx = lax.axis_index("ctx")
    head = lax.axis_index("head")
    other = 1 - sub

    def cols(c):
        return pl.ds(pl.multiple_of(c * CHUNK, CHUNK), CHUNK)

    loads = [
        pltpu.make_async_copy(g_hbm.at[:, pl.ds(pl.multiple_of(sub * HP, 128), HP)], g_v, ld_sem.at[0]),
        pltpu.make_async_copy(x_hbm, x_v, ld_sem.at[1]),
        pltpu.make_async_copy(w_hbm.at[:, pl.ds(pl.multiple_of(sub * HP, 128), HP)], wa_v, ld_sem.at[2]),
    ]
    for k in range(NH):
        loads.append(pltpu.make_async_copy(
            w_hbm.at[pl.ds(pl.multiple_of((k * NS + sub) * OC, 128), OC), :], wb_v.at[k], ld_sem.at[3 + k]))
    for ld in loads:
        ld.start()

    barrier = pltpu.get_barrier_semaphore()
    count = NH * NS - 1
    for dh in range(NH):
        for ds in range(NS):
            if dh or ds:
                pl.semaphore_signal(barrier, inc=1, device_id={
                    "head": lax.rem(head + dh, NH), "sub": lax.rem(sub + ds, NS)}, device_id_type=MESH)
    for l in range(LV):
        hop = 2 ** l
        up, down = ctx + hop < NCTX, ctx - hop >= 0
        count = count + up.astype(jnp.int32) + down.astype(jnp.int32)

        @pl.when(up)
        def _():
            pl.semaphore_signal(barrier, inc=1, device_id={"ctx": ctx + hop}, device_id_type=MESH)

        @pl.when(down)
        def _():
            pl.semaphore_signal(barrier, inc=1, device_id={"ctx": ctx - hop}, device_id_type=MESH)
    pl.semaphore_wait(barrier, count)

    bc_copies = [remote(b_ref, b_oth, bc_sem, 0, {"sub": other}), remote(c_ref, c_oth, bc_sem, 1, {"sub": other})]
    for cp in bc_copies:
        cp.start()

    def own_rows(v):
        r = v[:H]
        for k in range(1, NS):
            r = jnp.where(sub == k, v[k * H:(k + 1) * H], r)
        return r

    rows = [own_rows(dec_ref[...])] + [own_rows(lw_ref[l]) for l in range(LV + 1)]
    used = H * len(rows)
    stacked = jnp.concatenate(rows + [jnp.zeros((128 - used, T), F32)], axis=0)
    turned = jnp.transpose(stacked)
    dec_t = turned[:, :H]
    lam_t = turned[:, H:2 * H]
    r_i = lax.broadcasted_iota(jnp.int32, (T, T), 0)
    c_i = lax.broadcasted_iota(jnp.int32, (T, T), 1)
    tri = jnp.where(r_i >= c_i, 1.0, 0.0).astype(BF16)
    d1 = dec_t.astype(BF16)
    rest = dec_t - d1.astype(F32)
    d2 = rest.astype(BF16)
    d3 = (rest - d2.astype(F32)).astype(BF16)
    def halves(v):
        hi = v.astype(BF16)
        return jnp.concatenate([hi.astype(F32), v - hi.astype(F32)], axis=1).astype(BF16)

    cum_t = mm(tri, d1) + (mm(tri, d2) + mm(tri, d3))
    cum_r = jnp.transpose(jnp.concatenate([cum_t, jnp.zeros((T, 128 - H), F32)], axis=1))
    for c in range(nchunk):
        cumr_v[c, :hpc] = cum_r[c * hpc:(c + 1) * hpc]
        lam_v[c, :hpc] = rows[1][c * hpc:(c + 1) * hpc]
        cumc_v[c] = cum_t[:, c * hpc:(c + 1) * hpc]
    tot = cum_t[T - 1:T]
    grow = jnp.exp(cum_t)
    coef_v[0] = halves(jnp.exp(jnp.minimum(tot - cum_t, 0.0)))
    for l in range(LV):
        coef_v[1 + l] = halves(turned[:, (l + 2) * H:(l + 3) * H] * grow)
    ref_a = cum_t[half - 1:half]
    coef_v[1 + LV] = halves(jnp.concatenate([
        jnp.exp(jnp.minimum(ref_a - cum_t[:half], 0.0)),
        lam_t[half:] * jnp.exp(jnp.minimum(cum_t[half:] - ref_a, 0.0))], axis=0))
    pieces = []
    for base in (0, half):
        mid = base + quarter
        ref_b = cum_t[mid - 1:mid]
        pieces.append(jnp.exp(jnp.minimum(ref_b - cum_t[base:mid], 0.0)))
        pieces.append(lam_t[mid:mid + quarter] * jnp.exp(jnp.minimum(cum_t[mid:mid + quarter] - ref_b, 0.0)))
    coef_v[2 + LV] = halves(jnp.concatenate(pieces, axis=0))

    def selector(c, dtype):
        h_i = lax.broadcasted_iota(jnp.int32, (H, CHUNK), 0)
        l_i = lax.broadcasted_iota(jnp.int32, (H, CHUNK), 1)
        return jnp.where(h_i == c * hpc + lax.div(l_i, HD), 1.0, 0.0).astype(dtype)

    def spread(v, c):
        h_i = lax.rem(lax.broadcasted_iota(jnp.int32, (2 * H, CHUNK), 0), H)
        l_i = lax.broadcasted_iota(jnp.int32, (2 * H, CHUNK), 1)
        return mm(v, jnp.where(h_i == c * hpc + lax.div(l_i, HD), 1.0, 0.0).astype(BF16))

    tot8 = jnp.broadcast_to(tot, (8, H))
    t1 = tot8.astype(BF16)
    rest = tot8 - t1.astype(F32)
    t2 = rest.astype(BF16)
    t3 = (rest - t2.astype(F32)).astype(BF16)
    for c in range(nchunk):
        sel = selector(c, BF16)
        wlog[0, :, c * CHUNK:(c + 1) * CHUNK] = mm(t1, sel) + (mm(t2, sel) + mm(t3, sel))
    gap[0] = jnp.zeros((8, HP), F32)

    def shift(l, sign, src, dst, sems, idx):
        hop = sign * 2 ** l
        sends = (ctx + hop < NCTX) & (ctx + hop >= 0)
        gets = (ctx - hop < NCTX) & (ctx - hop >= 0)
        cp = remote(src, dst, sems, idx, {"ctx": ctx + hop})

        def start():
            pl.when(sends)(cp.start)

        def arrive():
            pl.when(gets)(cp.wait_recv)

            @pl.when(jnp.logical_not(gets))
            def _():
                dst[...] = jnp.zeros(dst.shape, dst.dtype)

        def end():
            pl.when(sends)(cp.wait_send)

        return start, arrive, end

    log_moves = [shift(l, 1, wlog.at[l], alog.at[l], log_sem, l) for l in range(LV - 1)]
    fwd = [shift(l, 1, win_s.at[l], arr_v.at[l], fwd_sem, l) for l in range(LV)]
    bwd = [shift(l, -1, ret_s.at[l], came_v.at[l], bwd_sem, l) for l in range(LV)]

    if LV > 1:
        log_moves[0][0]()

    for cp in bc_copies:
        cp.wait_recv()
    bt_v[:n_half] = b_ref[...]
    bt_v[n_half:] = b_oth[...]
    ct_v[:n_half] = c_ref[...]
    ct_v[n_half:] = c_oth[...]
    b_v[...] = jnp.transpose(bt_v[...].astype(F32)).astype(BF16)
    c_v[...] = jnp.transpose(ct_v[...].astype(F32)).astype(BF16)
    loads[0].wait()

    def level_grads(l):
        @pl.loop(0, nchunk)
        def _(c):
            gl = (g_v[:, cols(c)].astype(F32) * spread(coef_v[1 + l], c)).astype(BF16)
            gl_v[l, :, cols(c)] = gl
            a_v[l, :, cols(c)] = mm(ct_v[...], gl)

    level_grads(LV - 1)
    for l in range(LV - 1):
        log_moves[l][1]()
        gap[l + 1] = gap[l] + alog[l]
        wlog[l + 1] = wlog[l] + alog[l]
        if l + 1 < LV - 1:
            log_moves[l + 1][0]()
    ret_s[LV - 1] = (a_v[LV - 1] * jnp.exp(gap[LV - 1, 0:1])).astype(BF16)
    bwd[LV - 1][0]()

    for l in range(LV - 1):
        level_grads(l)

    loads[1].wait()
    loads[2].wait()

    @pl.loop(0, nchunk)
    def _(c):
        proj = mm(x_v[...], wa_v[:, cols(c)]).astype(BF16)
        p_v[:, cols(c)] = proj
        pe = (proj.astype(F32) * spread(coef_v[0], c)).astype(BF16)
        pe_v[:, cols(c)] = pe
        e = mm(bt_v[...], pe)
        e_v[:, cols(c)] = e
        win_s[0, :, cols(c)] = e.astype(BF16)

    fwd[0][0]()

    sc_v[...] = mm_nt(b_v[...], c_v[...])
    scb_v[...] = sc_v[...].astype(BF16)
    z_v[...] = jnp.zeros((T, T), F32)

    def off_block(c, coef, u0, t0, size):
        us, ts = slice(u0, u0 + size), slice(t0, t0 + size)
        eb = spread(coef_v[coef, us], c)
        ga = (g_v[ts, cols(c)].astype(F32) * spread(coef_v[coef, ts], c)).astype(BF16)
        pb = (p_v[us, cols(c)].astype(F32) * eb).astype(BF16)
        z_v[us, ts] += mm_nt(pb, ga)
        return eb * mm(scb_v[us, ts], ga)

    @pl.loop(0, nchunk)
    def _(c):
        far = off_block(c, 1 + LV, 0, half, half)
        near_a = off_block(c, 2 + LV, 0, quarter, quarter)
        near_b = off_block(c, 2 + LV, half, half + quarter, quarter)
        gxl_v[:half, cols(c)] = far
        gxl_v[:quarter, cols(c)] += near_a
        gxl_v[half:half + quarter, cols(c)] = near_b
        gxl_v[quarter * 3:, cols(c)] = jnp.zeros((quarter, CHUNK), F32)

    for l in range(LV - 1):
        k = LV - 1 - l
        bwd[k][1]()
        if l == 0:
            sg_v[...] = came_v[k].astype(F32)
        else:
            sg_v[...] += came_v[k].astype(F32)
        ret_s[k - 1] = (a_v[k - 1] * jnp.exp(gap[k - 1, 0:1])
                        + jnp.exp(wlog[k - 1, 0:1]) * sg_v[...]).astype(BF16)
        bwd[k - 1][0]()
        fwd[l][1]()
        e_v[...] += jnp.exp(wlog[l, 0:1]) * arr_v[l].astype(F32)
        win_s[l + 1] = e_v[...].astype(BF16)
        fwd[l + 1][0]()

    q_r = lax.broadcasted_iota(jnp.int32, (quarter, quarter), 0)
    q_c = lax.broadcasted_iota(jnp.int32, (quarter, quarter), 1)

    m_c = lax.div(lax.broadcasted_iota(jnp.int32, (quarter, CHUNK), 1), HD)
    masks = [jnp.where(m_c == j, 1.0, 0.0).astype(BF16) for j in range(hpc)]

    keep = q_c >= q_r

    def diagonal(blocks):
        @pl.loop(0, nchunk)
        def _(c):
            for i in blocks:
                sl = slice(i * quarter, (i + 1) * quarter)
                p_b, g_b = p_v[sl, cols(c)], g_v[sl, cols(c)]
                dots = mm_nt(jnp.concatenate([p_b * m for m in masks], axis=0), g_b)
                zsum = z_v[sl, sl]
                weights = []
                for j in range(hpc):
                    row = cumr_v[c, j:j + 1, sl]
                    lam = lam_v[c, j:j + 1, sl]
                    col = cumc_v[c, sl, j:j + 1]
                    dec = jnp.where(keep, jnp.exp(row - col) * lam, 0.0)
                    zsum = zsum + dec * dots[j * quarter:(j + 1) * quarter]
                    weights.append((dec * sc_v[sl, sl]).astype(BF16))
                z_v[sl, sl] = zsum
                gxl_v[sl, cols(c)] += mm(jnp.concatenate(weights, axis=1),
                                         jnp.concatenate([g_b * m for m in masks], axis=0))

    diagonal((0, 1))

    bwd[0][1]()
    if LV > 1:
        sg_v[...] += came_v[0].astype(F32)
    else:
        sg_v[...] = came_v[0].astype(F32)
    sgb = sg_v[...].astype(BF16)
    came_v[0] = sgb
    gx_copies, part_copies = [], []

    def send_rows(r):
        rs = slice(r * blk, (r + 1) * blk)

        @pl.loop(0, nchunk)
        def _(c):
            ew = spread(coef_v[0, rs], c)
            gx = gxl_v[rs, cols(c)] + ew * mm(b_v[rs], came_v[0, :, cols(c)])
            gx_v[sub, rs, cols(c)] = gx.astype(BF16)

        cp = remote(gx_v.at[sub, pl.ds(r * blk, blk)], gx_v.at[sub, pl.ds(r * blk, blk)], gx_sem, r, {"sub": other})
        cp.start()
        gx_copies.append(cp)

    def send_parts(r):
        rs = slice(r * blk, (r + 1) * blk)
        gx_copies[r].wait_recv()
        for d in range(1, NH):
            k = lax.rem(head + d, NH)
            part = mm_nt(gx_v[0, rs], wb_v[k, :, :HP]) + mm_nt(gx_v[1, rs], wb_v[k, :, HP:])
            part_s[d - 1, rs] = part.astype(BF16)
            cp = remote(part_s.at[d - 1, pl.ds(r * blk, blk)], part_r.at[d - 1, pl.ds(r * blk, blk)],
                        part_sem, (d - 1) * RB + r, {"head": k})
            cp.start()
            part_copies.append(cp)

    send_rows(0)
    diagonal((2, 3))
    for k in range(NH):
        loads[3 + k].wait()
    send_parts(0)
    send_rows(1)
    gb_all = mm(z_v[...].astype(BF16), c_v[...]) + mm_nt(pe_v[...], came_v[0])
    gc_all = mm(jnp.transpose(z_v[...]).astype(BF16), b_v[...])
    send_parts(1)

    fwd[LV - 1][1]()
    for l in range(LV):
        gc_all = gc_all + mm_nt(gl_v[l], (arr_v[l].astype(F32) * jnp.exp(gap[l, 0:1])).astype(BF16))
    gbc_copies = []
    gbc_s[0, 0] = gb_all[:, :n_half].astype(BF16)
    gbc_s[0, 1] = gc_all[:, :n_half].astype(BF16)
    gbc_s[1, 0] = gb_all[:, n_half:].astype(BF16)
    gbc_s[1, 1] = gc_all[:, n_half:].astype(BF16)
    for dh in range(NH):
        for ds in range(NS):
            if dh or ds:
                k = lax.rem(head + dh, NH)
                n = dh * NS + ds - 1
                cp = remote(gbc_s.at[ds, :, pl.ds(pl.multiple_of(k * tok_own, 16), tok_own)], gbc_r.at[n],
                            gbc_sem, n, {"head": k, "sub": lax.rem(sub + ds, NS)})
                cp.start()
                gbc_copies.append(cp)
    own_v[...] = mm_nt(gx_v[0], wb_v[head, :, :HP]) + mm_nt(gx_v[1], wb_v[head, :, HP:])
    own_tok = pl.ds(pl.multiple_of(head * tok_own, 16), tok_own)
    gb = gbc_s[0, 0, own_tok].astype(F32)
    gc = gbc_s[0, 1, own_tok].astype(F32)
    for n, cp in enumerate(gbc_copies):
        cp.wait_recv()
        gb = gb + gbc_r[n, 0].astype(F32)
        gc = gc + gbc_r[n, 1].astype(F32)
    both = jnp.transpose(jnp.concatenate([gb, gc], axis=1))
    gb_ref[...] = both[:n_half].astype(BF16)
    gc_ref[...] = both[n_half:].astype(BF16)
    for r in range(RB):
        rs = slice(r * blk, (r + 1) * blk)
        acc = own_v[rs]
        for d in range(1, NH):
            part_copies[r * (NH - 1) + d - 1].wait_recv()
            acc = acc + part_r[d - 1, rs].astype(F32)
        out_ref[rs] = acc.astype(BF16)

    for cp in bc_copies + gx_copies + part_copies + gbc_copies:
        cp.wait_send()
    for mv in log_moves + fwd + bwd:
        mv[2]()


def hand_out(*refs):
    for src, dst in zip(refs[:3], refs[3:]):
        dst[...] = src[...]


def shards(inputs, w_in, b_in, c_in, log_decay, level_weight, out_grad):
    T, D = inputs.shape
    HG, inner = log_decay.shape[0], w_in.shape[1]
    HD = inner // HG
    NS, NH, NCTX = (lax.axis_size(a) for a in ("sub", "head", "ctx"))
    LV = level_weight.shape[0] - 1
    H = HG // NS
    HP = H * HD
    nh = b_in.shape[1]
    N = nh * NS
    OC = D // NH // NS
    RB = 2
    nchunk = HP // CHUNK
    tok_own = T // NH
    dims = (T, H, HP, HD, NS, NH, NCTX, LV, OC, RB)
    V = pltpu.VMEM
    scratch = [
        V((T, D), BF16), V((D, HP), BF16), V((NH, OC, inner), BF16), V((T, HP), BF16),
        V((nh, T), BF16), V((nh, T), BF16), V((T, N), BF16), V((T, N), BF16), V((N, T), BF16), V((N, T), BF16),
        V((LV + 3, T, 2 * H), BF16), V((nchunk, T, CHUNK // HD), F32), V((nchunk, 8, T), F32), V((nchunk, 8, T), F32),
        V((LV, 8, HP), F32), V((LV, 8, HP), F32), V((LV, 8, HP), F32),
        V((LV, T, HP), BF16), V((T, HP), BF16), V((T, HP), BF16), V((LV, N, HP), F32), V((N, HP), F32),
        V((LV, N, HP), BF16), V((LV, N, HP), BF16), V((LV, N, HP), BF16), V((LV, N, HP), BF16), V((N, HP), F32),
        V((T, T), F32), V((T, T), BF16), V((T, T), F32), V((T, HP), F32), V((NS, T, HP), BF16),
        V((NH - 1, T, OC), BF16), V((NH - 1, T, OC), BF16), V((T, OC), F32),
        V((NS, 2, T, nh), BF16), V((NH * NS - 1, 2, tok_own, nh), BF16),
    ]
    S = pltpu.SemaphoreType.DMA
    scratch += [S((3 + NH,)), S((2, 2)), S((2, LV)), S((2, LV)), S((2, LV)), S((2, RB)),
                S((2, (NH - 1) * RB)), S((2, NH * NS - 1))]
    vm = pl.BlockSpec(memory_space=pltpu.VMEM)
    hb = pl.BlockSpec(memory_space=pl.ANY)
    grad_inputs, grad_b, grad_c = pl.pallas_call(
        functools.partial(kernel, dims),
        out_shape=(jax.ShapeDtypeStruct((T, OC), BF16), jax.ShapeDtypeStruct((nh, tok_own), BF16),
                   jax.ShapeDtypeStruct((nh, tok_own), BF16)),
        in_specs=[hb, hb, hb, vm, vm, vm, vm],
        out_specs=(vm, vm, vm),
        scratch_shapes=scratch,
        compiler_params=pltpu.CompilerParams(
            collective_id=0, has_side_effects=True, vmem_limit_bytes=56 * 2 ** 20),
    )(inputs, w_in, out_grad, b_in.T, c_in.T, log_decay, level_weight)
    outs = (grad_inputs, grad_b, grad_c)
    grad_inputs, grad_b, grad_c = pl.pallas_call(
        hand_out, out_shape=tuple(jax.ShapeDtypeStruct(o.shape, o.dtype) for o in outs),
        in_specs=[vm] * 3, out_specs=(vm,) * 3)(*outs)
    return grad_inputs, grad_b.T, grad_c.T


def solution(mesh):
    in_specs = (
        P(("groups", "ctx"), None),
        P(None, "head"),
        P(("groups", "ctx"), "sub"),
        P(("groups", "ctx"), "sub"),
        P("head", ("groups", "ctx")),
        P(None, "head", ("groups", "ctx")),
        P(("groups", "ctx"), "head"),
    )
    out_specs = (
        P(("groups", "ctx"), ("head", "sub")),
        P(("groups", "ctx", "head"), "sub"),
        P(("groups", "ctx", "head"), "sub"),
    )
    return jax.shard_map(shards, mesh=mesh, in_specs=in_specs, out_specs=out_specs, check_vma=False)
```

```python
import functools
import jax
import jax.numpy as jnp
from jax import lax
from jax.experimental import pallas as pl
from jax.experimental.pallas import tpu as pltpu
from jax.sharding import PartitionSpec as P

F32, BF16 = jnp.float32, jnp.bfloat16
MESH = pl.DeviceIdType.MESH
CHUNK = 256


def mm(a, b):
    return lax.dot_general(a, b, (((1,), (0,)), ((), ())), preferred_element_type=F32)


def mm_nt(a, b):
    return lax.dot_general(a, b, (((1,), (1,)), ((), ())), preferred_element_type=F32)


def remote(src, dst, sems, idx, where):
    return pltpu.make_async_remote_copy(
        src_ref=src, dst_ref=dst, send_sem=sems.at[0, idx], recv_sem=sems.at[1, idx],
        device_id=where, device_id_type=MESH)


def kernel(dims, x_hbm, w_hbm, g_hbm, b_ref, c_ref, dec_ref, lw_ref,
           out_ref, gb_ref, gc_ref,
           x_v, wa_v, wb_v, g_v, b_oth, c_oth, b_v, c_v, bt_v, ct_v,
           coef_v, cumc_v, cumr_v, lam_v, wlog, alog, gap,
           gl_v, p_v, pe_v, a_v, e_v, win_s, arr_v, ret_s, came_v, sg_v,
           sc_v, scb_v, z_v, gxl_v, gx_v, part_s, part_r, own_v, gbc_s, gbc_r,
           ld_sem, bc_sem, log_sem, fwd_sem, bwd_sem, gx_sem, part_sem, gbc_sem):
    T, H, HP, HD, NS, NH, NCTX, LV, OC, RB = dims
    half, quarter = T // 2, T // 4
    hpc = CHUNK // HD
    nchunk = HP // CHUNK
    n_half = b_ref.shape[0]
    N = n_half * NS
    tok_own = T // NH
    blk = T // RB
    sub = lax.axis_index("sub")
    ctx = lax.axis_index("ctx")
    head = lax.axis_index("head")
    other = 1 - sub

    def cols(c):
        return pl.ds(pl.multiple_of(c * CHUNK, CHUNK), CHUNK)

    loads = [
        pltpu.make_async_copy(g_hbm.at[:, pl.ds(pl.multiple_of(sub * HP, 128), HP)], g_v, ld_sem.at[0]),
        pltpu.make_async_copy(x_hbm, x_v, ld_sem.at[1]),
        pltpu.make_async_copy(w_hbm.at[:, pl.ds(pl.multiple_of(sub * HP, 128), HP)], wa_v, ld_sem.at[2]),
    ]
    for k in range(NH):
        loads.append(pltpu.make_async_copy(
            w_hbm.at[pl.ds(pl.multiple_of((k * NS + sub) * OC, 128), OC), :], wb_v.at[k], ld_sem.at[3 + k]))
    for ld in loads[:3]:
        ld.start()

    barrier = pltpu.get_barrier_semaphore()
    count = NH * NS - 1
    for dh in range(NH):
        for ds in range(NS):
            if dh or ds:
                pl.semaphore_signal(barrier, inc=1, device_id={
                    "head": lax.rem(head + dh, NH), "sub": lax.rem(sub + ds, NS)}, device_id_type=MESH)
    for l in range(LV):
        hop = 2 ** l
        up, down = ctx + hop < NCTX, ctx - hop >= 0
        count = count + up.astype(jnp.int32) + down.astype(jnp.int32)

        @pl.when(up)
        def _():
            pl.semaphore_signal(barrier, inc=1, device_id={"ctx": ctx + hop}, device_id_type=MESH)

        @pl.when(down)
        def _():
            pl.semaphore_signal(barrier, inc=1, device_id={"ctx": ctx - hop}, device_id_type=MESH)
    pl.semaphore_wait(barrier, count)

    bc_copies = [remote(b_ref, b_oth, bc_sem, 0, {"sub": other}), remote(c_ref, c_oth, bc_sem, 1, {"sub": other})]
    for cp in bc_copies:
        cp.start()

    def own_rows(v):
        r = v[:H]
        for k in range(1, NS):
            r = jnp.where(sub == k, v[k * H:(k + 1) * H], r)
        return r

    rows = [own_rows(dec_ref[...])] + [own_rows(lw_ref[l]) for l in range(LV + 1)]
    used = H * len(rows)
    stacked = jnp.concatenate(rows + [jnp.zeros((128 - used, T), F32)], axis=0)
    turned = jnp.transpose(stacked)
    dec_t = turned[:, :H]
    lam_t = turned[:, H:2 * H]
    r_i = lax.broadcasted_iota(jnp.int32, (T, T), 0)
    c_i = lax.broadcasted_iota(jnp.int32, (T, T), 1)
    tri = jnp.where(r_i >= c_i, 1.0, 0.0).astype(BF16)
    d1 = dec_t.astype(BF16)
    rest = dec_t - d1.astype(F32)
    d2 = rest.astype(BF16)
    d3 = (rest - d2.astype(F32)).astype(BF16)
    def halves(v):
        hi = v.astype(BF16)
        return jnp.concatenate([hi.astype(F32), v - hi.astype(F32)], axis=1).astype(BF16)

    cum_t = mm(tri, d1) + (mm(tri, d2) + mm(tri, d3))
    cum_r = jnp.transpose(jnp.concatenate([cum_t, jnp.zeros((T, 128 - H), F32)], axis=1))
    for c in range(nchunk):
        cumr_v[c, :hpc] = cum_r[c * hpc:(c + 1) * hpc]
        lam_v[c, :hpc] = rows[1][c * hpc:(c + 1) * hpc]
        cumc_v[c] = cum_t[:, c * hpc:(c + 1) * hpc]
    tot = cum_t[T - 1:T]
    grow = jnp.exp(cum_t)
    coef_v[0] = halves(jnp.exp(jnp.minimum(tot - cum_t, 0.0)))
    for l in range(LV):
        coef_v[1 + l] = halves(turned[:, (l + 2) * H:(l + 3) * H] * grow)
    ref_a = cum_t[half - 1:half]
    coef_v[1 + LV] = halves(jnp.concatenate([
        jnp.exp(jnp.minimum(ref_a - cum_t[:half], 0.0)),
        lam_t[half:] * jnp.exp(jnp.minimum(cum_t[half:] - ref_a, 0.0))], axis=0))
    pieces = []
    for base in (0, half):
        mid = base + quarter
        ref_b = cum_t[mid - 1:mid]
        pieces.append(jnp.exp(jnp.minimum(ref_b - cum_t[base:mid], 0.0)))
        pieces.append(lam_t[mid:mid + quarter] * jnp.exp(jnp.minimum(cum_t[mid:mid + quarter] - ref_b, 0.0)))
    coef_v[2 + LV] = halves(jnp.concatenate(pieces, axis=0))

    def selector(c, dtype):
        h_i = lax.broadcasted_iota(jnp.int32, (H, CHUNK), 0)
        l_i = lax.broadcasted_iota(jnp.int32, (H, CHUNK), 1)
        return jnp.where(h_i == c * hpc + lax.div(l_i, HD), 1.0, 0.0).astype(dtype)

    def spread(v, c):
        h_i = lax.rem(lax.broadcasted_iota(jnp.int32, (2 * H, CHUNK), 0), H)
        l_i = lax.broadcasted_iota(jnp.int32, (2 * H, CHUNK), 1)
        return mm(v, jnp.where(h_i == c * hpc + lax.div(l_i, HD), 1.0, 0.0).astype(BF16))

    tot8 = jnp.broadcast_to(tot, (8, H))
    t1 = tot8.astype(BF16)
    rest = tot8 - t1.astype(F32)
    t2 = rest.astype(BF16)
    t3 = (rest - t2.astype(F32)).astype(BF16)
    for c in range(nchunk):
        sel = selector(c, BF16)
        wlog[0, :, c * CHUNK:(c + 1) * CHUNK] = mm(t1, sel) + (mm(t2, sel) + mm(t3, sel))
    gap[0] = jnp.zeros((8, HP), F32)

    def shift(l, sign, src, dst, sems, idx):
        hop = sign * 2 ** l
        sends = (ctx + hop < NCTX) & (ctx + hop >= 0)
        gets = (ctx - hop < NCTX) & (ctx - hop >= 0)
        cp = remote(src, dst, sems, idx, {"ctx": ctx + hop})

        def start():
            pl.when(sends)(cp.start)

        def arrive():
            pl.when(gets)(cp.wait_recv)

            @pl.when(jnp.logical_not(gets))
            def _():
                dst[...] = jnp.zeros(dst.shape, dst.dtype)

        def end():
            pl.when(sends)(cp.wait_send)

        return start, arrive, end

    log_moves = [shift(l, 1, wlog.at[l], alog.at[l], log_sem, l) for l in range(LV - 1)]
    fwd = [shift(l, 1, win_s.at[l], arr_v.at[l], fwd_sem, l) for l in range(LV)]
    bwd = [shift(l, -1, ret_s.at[l], came_v.at[l], bwd_sem, l) for l in range(LV)]

    if LV > 1:
        log_moves[0][0]()

    for cp in bc_copies:
        cp.wait_recv()
    bt_v[:n_half] = b_ref[...]
    bt_v[n_half:] = b_oth[...]
    ct_v[:n_half] = c_ref[...]
    ct_v[n_half:] = c_oth[...]
    b_v[...] = jnp.transpose(bt_v[...].astype(F32)).astype(BF16)
    c_v[...] = jnp.transpose(ct_v[...].astype(F32)).astype(BF16)
    loads[0].wait()

    def level_grads(l):
        @pl.loop(0, nchunk)
        def _(c):
            gl = (g_v[:, cols(c)].astype(F32) * spread(coef_v[1 + l], c)).astype(BF16)
            gl_v[l, :, cols(c)] = gl
            a_v[l, :, cols(c)] = mm(ct_v[...], gl)

    level_grads(LV - 1)
    for l in range(LV - 1):
        log_moves[l][1]()
        gap[l + 1] = gap[l] + alog[l]
        wlog[l + 1] = wlog[l] + alog[l]
        if l + 1 < LV - 1:
            log_moves[l + 1][0]()
    ret_s[LV - 1] = (a_v[LV - 1] * jnp.exp(gap[LV - 1, 0:1])).astype(BF16)
    bwd[LV - 1][0]()

    for l in range(LV - 1):
        level_grads(l)

    loads[1].wait()
    loads[2].wait()
    for ld in loads[3:]:
        ld.start()

    @pl.loop(0, nchunk)
    def _(c):
        proj = mm(x_v[...], wa_v[:, cols(c)]).astype(BF16)
        p_v[:, cols(c)] = proj
        pe = (proj.astype(F32) * spread(coef_v[0], c)).astype(BF16)
        pe_v[:, cols(c)] = pe
        e = mm(bt_v[...], pe)
        e_v[:, cols(c)] = e
        win_s[0, :, cols(c)] = e.astype(BF16)

    fwd[0][0]()

    sc_v[...] = mm_nt(b_v[...], c_v[...])
    scb_v[...] = sc_v[...].astype(BF16)
    z_v[...] = jnp.zeros((T, T), F32)

    def off_block(c, coef, u0, t0, size):
        us, ts = slice(u0, u0 + size), slice(t0, t0 + size)
        eb = spread(coef_v[coef, us], c)
        ga = (g_v[ts, cols(c)].astype(F32) * spread(coef_v[coef, ts], c)).astype(BF16)
        pb = (p_v[us, cols(c)].astype(F32) * eb).astype(BF16)
        z_v[us, ts] += mm_nt(pb, ga)
        return eb * mm(scb_v[us, ts], ga)

    @pl.loop(0, nchunk)
    def _(c):
        far = off_block(c, 1 + LV, 0, half, half)
        near_a = off_block(c, 2 + LV, 0, quarter, quarter)
        near_b = off_block(c, 2 + LV, half, half + quarter, quarter)
        gxl_v[:half, cols(c)] = far
        gxl_v[:quarter, cols(c)] += near_a
        gxl_v[half:half + quarter, cols(c)] = near_b
        gxl_v[quarter * 3:, cols(c)] = jnp.zeros((quarter, CHUNK), F32)

    q_r = lax.broadcasted_iota(jnp.int32, (quarter, quarter), 0)
    q_c = lax.broadcasted_iota(jnp.int32, (quarter, quarter), 1)

    m_c = lax.div(lax.broadcasted_iota(jnp.int32, (quarter, CHUNK), 1), HD)
    masks = [jnp.where(m_c == j, 1.0, 0.0).astype(BF16) for j in range(hpc)]

    keep = q_c >= q_r

    def diagonal(blocks):
        @pl.loop(0, nchunk)
        def _(c):
            for i in blocks:
                sl = slice(i * quarter, (i + 1) * quarter)
                p_b, g_b = p_v[sl, cols(c)], g_v[sl, cols(c)]
                dots = mm_nt(jnp.concatenate([p_b * m for m in masks], axis=0), g_b)
                zsum = z_v[sl, sl]
                weights = []
                for j in range(hpc):
                    row = cumr_v[c, j:j + 1, sl]
                    lam = lam_v[c, j:j + 1, sl]
                    col = cumc_v[c, sl, j:j + 1]
                    dec = jnp.where(keep, jnp.exp(row - col) * lam, 0.0)
                    zsum = zsum + dec * dots[j * quarter:(j + 1) * quarter]
                    weights.append((dec * sc_v[sl, sl]).astype(BF16))
                z_v[sl, sl] = zsum
                gxl_v[sl, cols(c)] += mm(jnp.concatenate(weights, axis=1),
                                         jnp.concatenate([g_b * m for m in masks], axis=0))

    for l in range(LV - 1):
        k = LV - 1 - l
        bwd[k][1]()
        if l == 0:
            sg_v[...] = came_v[k].astype(F32)
        else:
            sg_v[...] += came_v[k].astype(F32)
        ret_s[k - 1] = (a_v[k - 1] * jnp.exp(gap[k - 1, 0:1])
                        + jnp.exp(wlog[k - 1, 0:1]) * sg_v[...]).astype(BF16)
        bwd[k - 1][0]()
        if l == 0:
            diagonal((0, 1))
        fwd[l][1]()
        e_v[...] += jnp.exp(wlog[l, 0:1]) * arr_v[l].astype(F32)
        win_s[l + 1] = e_v[...].astype(BF16)
        fwd[l + 1][0]()
    if LV == 1:
        diagonal((0, 1))

    bwd[0][1]()
    if LV > 1:
        sg_v[...] += came_v[0].astype(F32)
    else:
        sg_v[...] = came_v[0].astype(F32)
    sgb = sg_v[...].astype(BF16)
    came_v[0] = sgb
    gx_copies, part_copies = [], []

    def send_rows(r):
        rs = slice(r * blk, (r + 1) * blk)

        @pl.loop(0, nchunk)
        def _(c):
            ew = spread(coef_v[0, rs], c)
            gx = gxl_v[rs, cols(c)] + ew * mm(b_v[rs], came_v[0, :, cols(c)])
            gx_v[sub, rs, cols(c)] = gx.astype(BF16)

        cp = remote(gx_v.at[sub, pl.ds(r * blk, blk)], gx_v.at[sub, pl.ds(r * blk, blk)], gx_sem, r, {"sub": other})
        cp.start()
        gx_copies.append(cp)

    def send_parts(r):
        rs = slice(r * blk, (r + 1) * blk)
        gx_copies[r].wait_recv()
        for d in range(1, NH):
            k = lax.rem(head + d, NH)
            part = mm_nt(gx_v[0, rs], wb_v[k, :, :HP]) + mm_nt(gx_v[1, rs], wb_v[k, :, HP:])
            part_s[d - 1, rs] = part.astype(BF16)
            cp = remote(part_s.at[d - 1, pl.ds(r * blk, blk)], part_r.at[d - 1, pl.ds(r * blk, blk)],
                        part_sem, (d - 1) * RB + r, {"head": k})
            cp.start()
            part_copies.append(cp)

    send_rows(0)
    diagonal((2, 3))
    for k in range(NH):
        loads[3 + k].wait()
    send_parts(0)
    send_rows(1)
    gb_all = mm(z_v[...].astype(BF16), c_v[...]) + mm_nt(pe_v[...], came_v[0])
    gc_all = mm(jnp.transpose(z_v[...]).astype(BF16), b_v[...])
    send_parts(1)

    fwd[LV - 1][1]()
    for l in range(LV):
        gc_all = gc_all + mm_nt(gl_v[l], (arr_v[l].astype(F32) * jnp.exp(gap[l, 0:1])).astype(BF16))
    gbc_copies = []
    gbc_s[0, 0] = gb_all[:, :n_half].astype(BF16)
    gbc_s[0, 1] = gc_all[:, :n_half].astype(BF16)
    gbc_s[1, 0] = gb_all[:, n_half:].astype(BF16)
    gbc_s[1, 1] = gc_all[:, n_half:].astype(BF16)
    for dh in range(NH):
        for ds in range(NS):
            if dh or ds:
                k = lax.rem(head + dh, NH)
                n = dh * NS + ds - 1
                cp = remote(gbc_s.at[ds, :, pl.ds(pl.multiple_of(k * tok_own, 16), tok_own)], gbc_r.at[n],
                            gbc_sem, n, {"head": k, "sub": lax.rem(sub + ds, NS)})
                cp.start()
                gbc_copies.append(cp)
    own_v[...] = mm_nt(gx_v[0], wb_v[head, :, :HP]) + mm_nt(gx_v[1], wb_v[head, :, HP:])
    own_tok = pl.ds(pl.multiple_of(head * tok_own, 16), tok_own)
    gb = gbc_s[0, 0, own_tok].astype(F32)
    gc = gbc_s[0, 1, own_tok].astype(F32)
    for n, cp in enumerate(gbc_copies):
        cp.wait_recv()
        gb = gb + gbc_r[n, 0].astype(F32)
        gc = gc + gbc_r[n, 1].astype(F32)
    both = jnp.transpose(jnp.concatenate([gb, gc], axis=1))
    gb_ref[...] = both[:n_half].astype(BF16)
    gc_ref[...] = both[n_half:].astype(BF16)
    for r in range(RB):
        rs = slice(r * blk, (r + 1) * blk)
        acc = own_v[rs]
        for d in range(1, NH):
            part_copies[r * (NH - 1) + d - 1].wait_recv()
            acc = acc + part_r[d - 1, rs].astype(F32)
        out_ref[rs] = acc.astype(BF16)

    for cp in bc_copies + gx_copies + part_copies + gbc_copies:
        cp.wait_send()
    for mv in log_moves + fwd + bwd:
        mv[2]()


def hand_out(*refs):
    for src, dst in zip(refs[:3], refs[3:]):
        dst[...] = src[...]


def shards(inputs, w_in, b_in, c_in, log_decay, level_weight, out_grad):
    T, D = inputs.shape
    HG, inner = log_decay.shape[0], w_in.shape[1]
    HD = inner // HG
    NS, NH, NCTX = (lax.axis_size(a) for a in ("sub", "head", "ctx"))
    LV = level_weight.shape[0] - 1
    H = HG // NS
    HP = H * HD
    nh = b_in.shape[1]
    N = nh * NS
    OC = D // NH // NS
    RB = 2
    nchunk = HP // CHUNK
    tok_own = T // NH
    dims = (T, H, HP, HD, NS, NH, NCTX, LV, OC, RB)
    V = pltpu.VMEM
    scratch = [
        V((T, D), BF16), V((D, HP), BF16), V((NH, OC, inner), BF16), V((T, HP), BF16),
        V((nh, T), BF16), V((nh, T), BF16), V((T, N), BF16), V((T, N), BF16), V((N, T), BF16), V((N, T), BF16),
        V((LV + 3, T, 2 * H), BF16), V((nchunk, T, CHUNK // HD), F32), V((nchunk, 8, T), F32), V((nchunk, 8, T), F32),
        V((LV, 8, HP), F32), V((LV, 8, HP), F32), V((LV, 8, HP), F32),
        V((LV, T, HP), BF16), V((T, HP), BF16), V((T, HP), BF16), V((LV, N, HP), F32), V((N, HP), F32),
        V((LV, N, HP), BF16), V((LV, N, HP), BF16), V((LV, N, HP), BF16), V((LV, N, HP), BF16), V((N, HP), F32),
        V((T, T), F32), V((T, T), BF16), V((T, T), F32), V((T, HP), F32), V((NS, T, HP), BF16),
        V((NH - 1, T, OC), BF16), V((NH - 1, T, OC), BF16), V((T, OC), F32),
        V((NS, 2, T, nh), BF16), V((NH * NS - 1, 2, tok_own, nh), BF16),
    ]
    S = pltpu.SemaphoreType.DMA
    scratch += [S((3 + NH,)), S((2, 2)), S((2, LV)), S((2, LV)), S((2, LV)), S((2, RB)),
                S((2, (NH - 1) * RB)), S((2, NH * NS - 1))]
    vm = pl.BlockSpec(memory_space=pltpu.VMEM)
    hb = pl.BlockSpec(memory_space=pl.ANY)
    grad_inputs, grad_b, grad_c = pl.pallas_call(
        functools.partial(kernel, dims),
        out_shape=(jax.ShapeDtypeStruct((T, OC), BF16), jax.ShapeDtypeStruct((nh, tok_own), BF16),
                   jax.ShapeDtypeStruct((nh, tok_own), BF16)),
        in_specs=[hb, hb, hb, vm, vm, vm, vm],
        out_specs=(vm, vm, vm),
        scratch_shapes=scratch,
        compiler_params=pltpu.CompilerParams(
            collective_id=0, has_side_effects=True, vmem_limit_bytes=56 * 2 ** 20),
    )(inputs, w_in, out_grad, b_in.T, c_in.T, log_decay, level_weight)
    outs = (grad_inputs, grad_b, grad_c)
    grad_inputs, grad_b, grad_c = pl.pallas_call(
        hand_out, out_shape=tuple(jax.ShapeDtypeStruct(o.shape, o.dtype) for o in outs),
        in_specs=[vm] * 3, out_specs=(vm,) * 3)(*outs)
    return grad_inputs, grad_b.T, grad_c.T


def solution(mesh):
    in_specs = (
        P(("groups", "ctx"), None),
        P(None, "head"),
        P(("groups", "ctx"), "sub"),
        P(("groups", "ctx"), "sub"),
        P("head", ("groups", "ctx")),
        P(None, "head", ("groups", "ctx")),
        P(("groups", "ctx"), "head"),
    )
    out_specs = (
        P(("groups", "ctx"), ("head", "sub")),
        P(("groups", "ctx", "head"), "sub"),
        P(("groups", "ctx", "head"), "sub"),
    )
    return jax.shard_map(shards, mesh=mesh, in_specs=in_specs, out_specs=out_specs, check_vma=False)
```

```python
import functools
import jax
import jax.numpy as jnp
from jax import lax
from jax.experimental import pallas as pl
from jax.experimental.pallas import tpu as pltpu
from jax.sharding import PartitionSpec as P

F32, BF16 = jnp.float32, jnp.bfloat16
MESH = pl.DeviceIdType.MESH
CHUNK = 256


def mm(a, b):
    return lax.dot_general(a, b, (((1,), (0,)), ((), ())), preferred_element_type=F32)


def mm_nt(a, b):
    return lax.dot_general(a, b, (((1,), (1,)), ((), ())), preferred_element_type=F32)


def remote(src, dst, sems, idx, where):
    return pltpu.make_async_remote_copy(
        src_ref=src, dst_ref=dst, send_sem=sems.at[0, idx], recv_sem=sems.at[1, idx],
        device_id=where, device_id_type=MESH)


def kernel(dims, x_hbm, w_hbm, g_hbm, b_ref, c_ref, dec_ref, lw_ref,
           out_ref, gb_ref, gc_ref,
           x_v, wa_v, wb_v, g_v, b_oth, c_oth, b_v, c_v, bt_v, ct_v,
           coef_v, cumc_v, cumr_v, lam_v, wlog, alog, gap,
           gl_v, p_v, pe_v, a_v, e_v, win_s, arr_v, ret_s, came_v, sg_v,
           sc_v, scb_v, z_v, gxl_v, gx_v, part_s, part_r, own_v, gbc_s, gbc_r,
           ld_sem, bc_sem, log_sem, fwd_sem, bwd_sem, gx_sem, part_sem, gbc_sem):
    T, H, HP, HD, NS, NH, NCTX, LV, OC, RB = dims
    half, quarter = T // 2, T // 4
    hpc = CHUNK // HD
    nchunk = HP // CHUNK
    n_half = b_ref.shape[0]
    N = n_half * NS
    tok_own = T // NH
    blk = T // RB
    sub = lax.axis_index("sub")
    ctx = lax.axis_index("ctx")
    head = lax.axis_index("head")
    other = 1 - sub

    def cols(c):
        return pl.ds(pl.multiple_of(c * CHUNK, CHUNK), CHUNK)

    loads = [
        pltpu.make_async_copy(g_hbm.at[:, pl.ds(pl.multiple_of(sub * HP, 128), HP)], g_v, ld_sem.at[0]),
        pltpu.make_async_copy(x_hbm, x_v, ld_sem.at[1]),
        pltpu.make_async_copy(w_hbm.at[:, pl.ds(pl.multiple_of(sub * HP, 128), HP)], wa_v, ld_sem.at[2]),
    ]
    for k in range(NH):
        loads.append(pltpu.make_async_copy(
            w_hbm.at[pl.ds(pl.multiple_of((k * NS + sub) * OC, 128), OC), :], wb_v.at[k], ld_sem.at[3 + k]))
    for ld in loads[:3]:
        ld.start()

    barrier = pltpu.get_barrier_semaphore()
    count = NH * NS - 1
    for dh in range(NH):
        for ds in range(NS):
            if dh or ds:
                pl.semaphore_signal(barrier, inc=1, device_id={
                    "head": lax.rem(head + dh, NH), "sub": lax.rem(sub + ds, NS)}, device_id_type=MESH)
    for l in range(LV):
        hop = 2 ** l
        up, down = ctx + hop < NCTX, ctx - hop >= 0
        count = count + up.astype(jnp.int32) + down.astype(jnp.int32)

        @pl.when(up)
        def _():
            pl.semaphore_signal(barrier, inc=1, device_id={"ctx": ctx + hop}, device_id_type=MESH)

        @pl.when(down)
        def _():
            pl.semaphore_signal(barrier, inc=1, device_id={"ctx": ctx - hop}, device_id_type=MESH)
    pl.semaphore_wait(barrier, count)

    bc_copies = [remote(b_ref, b_oth, bc_sem, 0, {"sub": other}), remote(c_ref, c_oth, bc_sem, 1, {"sub": other})]
    for cp in bc_copies:
        cp.start()

    def own_rows(v):
        r = v[:H]
        for k in range(1, NS):
            r = jnp.where(sub == k, v[k * H:(k + 1) * H], r)
        return r

    rows = [own_rows(dec_ref[...])] + [own_rows(lw_ref[l]) for l in range(LV + 1)]
    used = H * len(rows)
    stacked = jnp.concatenate(rows + [jnp.zeros((128 - used, T), F32)], axis=0)
    turned = jnp.transpose(stacked)
    dec_t = turned[:, :H]
    lam_t = turned[:, H:2 * H]
    r_i = lax.broadcasted_iota(jnp.int32, (T, T), 0)
    c_i = lax.broadcasted_iota(jnp.int32, (T, T), 1)
    tri = jnp.where(r_i >= c_i, 1.0, 0.0).astype(BF16)
    d1 = dec_t.astype(BF16)
    rest = dec_t - d1.astype(F32)
    d2 = rest.astype(BF16)
    d3 = (rest - d2.astype(F32)).astype(BF16)
    def halves(v):
        hi = v.astype(BF16)
        return jnp.concatenate([hi.astype(F32), v - hi.astype(F32)], axis=1).astype(BF16)

    cum_t = mm(tri, d1) + (mm(tri, d2) + mm(tri, d3))
    cum_r = jnp.transpose(jnp.concatenate([cum_t, jnp.zeros((T, 128 - H), F32)], axis=1))
    for c in range(nchunk):
        cumr_v[c, :hpc] = cum_r[c * hpc:(c + 1) * hpc]
        lam_v[c, :hpc] = rows[1][c * hpc:(c + 1) * hpc]
        cumc_v[c] = cum_t[:, c * hpc:(c + 1) * hpc]
    tot = cum_t[T - 1:T]
    grow = jnp.exp(cum_t)
    coef_v[0] = halves(jnp.exp(jnp.minimum(tot - cum_t, 0.0)))
    for l in range(LV):
        coef_v[1 + l] = halves(turned[:, (l + 2) * H:(l + 3) * H] * grow)
    ref_a = cum_t[half - 1:half]
    coef_v[1 + LV] = halves(jnp.concatenate([
        jnp.exp(jnp.minimum(ref_a - cum_t[:half], 0.0)),
        lam_t[half:] * jnp.exp(jnp.minimum(cum_t[half:] - ref_a, 0.0))], axis=0))
    pieces = []
    for base in (0, half):
        mid = base + quarter
        ref_b = cum_t[mid - 1:mid]
        pieces.append(jnp.exp(jnp.minimum(ref_b - cum_t[base:mid], 0.0)))
        pieces.append(lam_t[mid:mid + quarter] * jnp.exp(jnp.minimum(cum_t[mid:mid + quarter] - ref_b, 0.0)))
    coef_v[2 + LV] = halves(jnp.concatenate(pieces, axis=0))

    def selector(c, dtype):
        h_i = lax.broadcasted_iota(jnp.int32, (H, CHUNK), 0)
        l_i = lax.broadcasted_iota(jnp.int32, (H, CHUNK), 1)
        return jnp.where(h_i == c * hpc + lax.div(l_i, HD), 1.0, 0.0).astype(dtype)

    def spread(v, c):
        h_i = lax.rem(lax.broadcasted_iota(jnp.int32, (2 * H, CHUNK), 0), H)
        l_i = lax.broadcasted_iota(jnp.int32, (2 * H, CHUNK), 1)
        return mm(v, jnp.where(h_i == c * hpc + lax.div(l_i, HD), 1.0, 0.0).astype(BF16))

    tot8 = jnp.broadcast_to(tot, (8, H))
    t1 = tot8.astype(BF16)
    rest = tot8 - t1.astype(F32)
    t2 = rest.astype(BF16)
    t3 = (rest - t2.astype(F32)).astype(BF16)
    for c in range(nchunk):
        sel = selector(c, BF16)
        wlog[0, :, c * CHUNK:(c + 1) * CHUNK] = mm(t1, sel) + (mm(t2, sel) + mm(t3, sel))
    gap[0] = jnp.zeros((8, HP), F32)

    def shift(l, sign, src, dst, sems, idx):
        hop = sign * 2 ** l
        sends = (ctx + hop < NCTX) & (ctx + hop >= 0)
        gets = (ctx - hop < NCTX) & (ctx - hop >= 0)
        cp = remote(src, dst, sems, idx, {"ctx": ctx + hop})

        def start():
            pl.when(sends)(cp.start)

        def arrive():
            pl.when(gets)(cp.wait_recv)

            @pl.when(jnp.logical_not(gets))
            def _():
                dst[...] = jnp.zeros(dst.shape, dst.dtype)

        def end():
            pl.when(sends)(cp.wait_send)

        return start, arrive, end

    log_moves = [shift(l, 1, wlog.at[l], alog.at[l], log_sem, l) for l in range(LV - 1)]
    fwd = [shift(l, 1, win_s.at[l], arr_v.at[l], fwd_sem, l) for l in range(LV)]
    bwd = [shift(l, -1, ret_s.at[l], came_v.at[l], bwd_sem, l) for l in range(LV)]

    if LV > 1:
        log_moves[0][0]()

    for cp in bc_copies:
        cp.wait_recv()
    bt_v[:n_half] = b_ref[...]
    bt_v[n_half:] = b_oth[...]
    ct_v[:n_half] = c_ref[...]
    ct_v[n_half:] = c_oth[...]
    b_v[...] = jnp.transpose(bt_v[...].astype(F32)).astype(BF16)
    c_v[...] = jnp.transpose(ct_v[...].astype(F32)).astype(BF16)
    loads[0].wait()

    def level_grads(l):
        @pl.loop(0, nchunk)
        def _(c):
            gl = (g_v[:, cols(c)].astype(F32) * spread(coef_v[1 + l], c)).astype(BF16)
            gl_v[l, :, cols(c)] = gl
            a_v[l, :, cols(c)] = mm(ct_v[...], gl)

    level_grads(LV - 1)
    for l in range(LV - 1):
        log_moves[l][1]()
        gap[l + 1] = gap[l] + alog[l]
        wlog[l + 1] = wlog[l] + alog[l]
        if l + 1 < LV - 1:
            log_moves[l + 1][0]()
    ret_s[LV - 1] = (a_v[LV - 1] * jnp.exp(gap[LV - 1, 0:1])).astype(BF16)
    bwd[LV - 1][0]()

    for l in range(LV - 1):
        level_grads(l)

    loads[1].wait()
    loads[2].wait()
    for ld in loads[3:]:
        ld.start()

    @pl.loop(0, nchunk)
    def _(c):
        proj = mm(x_v[...], wa_v[:, cols(c)]).astype(BF16)
        p_v[:, cols(c)] = proj
        pe = (proj.astype(F32) * spread(coef_v[0], c)).astype(BF16)
        pe_v[:, cols(c)] = pe
        e = mm(bt_v[...], pe)
        e_v[:, cols(c)] = e
        win_s[0, :, cols(c)] = e.astype(BF16)

    fwd[0][0]()

    sc_v[...] = mm_nt(b_v[...], c_v[...])
    scb_v[...] = sc_v[...].astype(BF16)
    z_v[...] = jnp.zeros((T, T), F32)

    def off_block(c, coef, u0, t0, size):
        us, ts = slice(u0, u0 + size), slice(t0, t0 + size)
        eb = spread(coef_v[coef, us], c)
        ga = (g_v[ts, cols(c)].astype(F32) * spread(coef_v[coef, ts], c)).astype(BF16)
        pb = (p_v[us, cols(c)].astype(F32) * eb).astype(BF16)
        z_v[us, ts] += mm_nt(pb, ga)
        return eb * mm(scb_v[us, ts], ga)

    @pl.loop(0, nchunk)
    def _(c):
        far = off_block(c, 1 + LV, 0, half, half)
        near_a = off_block(c, 2 + LV, 0, quarter, quarter)
        near_b = off_block(c, 2 + LV, half, half + quarter, quarter)
        gxl_v[:half, cols(c)] = far
        gxl_v[:quarter, cols(c)] += near_a
        gxl_v[half:half + quarter, cols(c)] = near_b
        gxl_v[quarter * 3:, cols(c)] = jnp.zeros((quarter, CHUNK), F32)

    q_r = lax.broadcasted_iota(jnp.int32, (quarter, quarter), 0)
    q_c = lax.broadcasted_iota(jnp.int32, (quarter, quarter), 1)

    m_c = lax.div(lax.broadcasted_iota(jnp.int32, (quarter, CHUNK), 1), HD)
    masks = [jnp.where(m_c == j, 1.0, 0.0).astype(BF16) for j in range(hpc)]

    keep = q_c >= q_r

    def diagonal(blocks):
        @pl.loop(0, nchunk)
        def _(c):
            for i in blocks:
                sl = slice(i * quarter, (i + 1) * quarter)
                p_b, g_b = p_v[sl, cols(c)], g_v[sl, cols(c)]
                dots = mm_nt(jnp.concatenate([p_b * m for m in masks], axis=0), g_b)
                zsum = z_v[sl, sl]
                weights = []
                for j in range(hpc):
                    row = cumr_v[c, j:j + 1, sl]
                    lam = lam_v[c, j:j + 1, sl]
                    col = cumc_v[c, sl, j:j + 1]
                    dec = jnp.where(keep, jnp.exp(row - col) * lam, 0.0)
                    zsum = zsum + dec * dots[j * quarter:(j + 1) * quarter]
                    weights.append((dec * sc_v[sl, sl]).astype(BF16))
                z_v[sl, sl] = zsum
                gxl_v[sl, cols(c)] += mm(jnp.concatenate(weights, axis=1),
                                         jnp.concatenate([g_b * m for m in masks], axis=0))

    for l in range(LV - 1):
        k = LV - 1 - l
        bwd[k][1]()
        if l == 0:
            sg_v[...] = came_v[k].astype(F32)
        else:
            sg_v[...] += came_v[k].astype(F32)
        ret_s[k - 1] = (a_v[k - 1] * jnp.exp(gap[k - 1, 0:1])
                        + jnp.exp(wlog[k - 1, 0:1]) * sg_v[...]).astype(BF16)
        bwd[k - 1][0]()
        if l == 0:
            diagonal((0, 1))
        fwd[l][1]()
        e_v[...] += jnp.exp(wlog[l, 0:1]) * arr_v[l].astype(F32)
        win_s[l + 1] = e_v[...].astype(BF16)
        fwd[l + 1][0]()
    if LV == 1:
        diagonal((0, 1))

    bwd[0][1]()
    if LV > 1:
        sg_v[...] += came_v[0].astype(F32)
    else:
        sg_v[...] = came_v[0].astype(F32)
    sgb = sg_v[...].astype(BF16)
    came_v[0] = sgb
    gx_copies, part_copies = [], []

    def send_rows(r):
        rs = slice(r * blk, (r + 1) * blk)

        @pl.loop(0, nchunk)
        def _(c):
            ew = spread(coef_v[0, rs], c)
            gx = gxl_v[rs, cols(c)] + ew * mm(b_v[rs], came_v[0, :, cols(c)])
            gx_v[sub, rs, cols(c)] = gx.astype(BF16)

        cp = remote(gx_v.at[sub, pl.ds(r * blk, blk)], gx_v.at[sub, pl.ds(r * blk, blk)], gx_sem, r, {"sub": other})
        cp.start()
        gx_copies.append(cp)

    def send_parts(r):
        rs = slice(r * blk, (r + 1) * blk)
        gx_copies[r].wait_recv()
        for d in range(1, NH):
            k = lax.rem(head + d, NH)
            part = mm_nt(gx_v[0, rs], wb_v[k, :, :HP]) + mm_nt(gx_v[1, rs], wb_v[k, :, HP:])
            part_s[d - 1, rs] = part.astype(BF16)
            cp = remote(part_s.at[d - 1, pl.ds(r * blk, blk)], part_r.at[d - 1, pl.ds(r * blk, blk)],
                        part_sem, (d - 1) * RB + r, {"head": k})
            cp.start()
            part_copies.append(cp)

    send_rows(0)
    send_rows(1)
    diagonal((2, 3))
    for k in range(NH):
        loads[3 + k].wait()
    send_parts(0)
    send_parts(1)
    send_rows(2)
    send_rows(3)
    gb_all = mm(z_v[...].astype(BF16), c_v[...]) + mm_nt(pe_v[...], came_v[0])
    gc_all = mm(jnp.transpose(z_v[...]).astype(BF16), b_v[...])
    send_parts(2)
    send_parts(3)

    fwd[LV - 1][1]()
    for l in range(LV):
        gc_all = gc_all + mm_nt(gl_v[l], (arr_v[l].astype(F32) * jnp.exp(gap[l, 0:1])).astype(BF16))
    gbc_copies = []
    gbc_s[0, 0] = gb_all[:, :n_half].astype(BF16)
    gbc_s[0, 1] = gc_all[:, :n_half].astype(BF16)
    gbc_s[1, 0] = gb_all[:, n_half:].astype(BF16)
    gbc_s[1, 1] = gc_all[:, n_half:].astype(BF16)
    for dh in range(NH):
        for ds in range(NS):
            if dh or ds:
                k = lax.rem(head + dh, NH)
                n = dh * NS + ds - 1
                cp = remote(gbc_s.at[ds, :, pl.ds(pl.multiple_of(k * tok_own, 16), tok_own)], gbc_r.at[n],
                            gbc_sem, n, {"head": k, "sub": lax.rem(sub + ds, NS)})
                cp.start()
                gbc_copies.append(cp)
    own_v[...] = mm_nt(gx_v[0], wb_v[head, :, :HP]) + mm_nt(gx_v[1], wb_v[head, :, HP:])
    own_tok = pl.ds(pl.multiple_of(head * tok_own, 16), tok_own)
    gb = gbc_s[0, 0, own_tok].astype(F32)
    gc = gbc_s[0, 1, own_tok].astype(F32)
    for n, cp in enumerate(gbc_copies):
        cp.wait_recv()
        gb = gb + gbc_r[n, 0].astype(F32)
        gc = gc + gbc_r[n, 1].astype(F32)
    both = jnp.transpose(jnp.concatenate([gb, gc], axis=1))
    gb_ref[...] = both[:n_half].astype(BF16)
    gc_ref[...] = both[n_half:].astype(BF16)
    for r in range(RB):
        rs = slice(r * blk, (r + 1) * blk)
        acc = own_v[rs]
        for d in range(1, NH):
            part_copies[r * (NH - 1) + d - 1].wait_recv()
            acc = acc + part_r[d - 1, rs].astype(F32)
        out_ref[rs] = acc.astype(BF16)

    for cp in bc_copies + gx_copies + part_copies + gbc_copies:
        cp.wait_send()
    for mv in log_moves + fwd + bwd:
        mv[2]()


def hand_out(*refs):
    for src, dst in zip(refs[:3], refs[3:]):
        dst[...] = src[...]


def shards(inputs, w_in, b_in, c_in, log_decay, level_weight, out_grad):
    T, D = inputs.shape
    HG, inner = log_decay.shape[0], w_in.shape[1]
    HD = inner // HG
    NS, NH, NCTX = (lax.axis_size(a) for a in ("sub", "head", "ctx"))
    LV = level_weight.shape[0] - 1
    H = HG // NS
    HP = H * HD
    nh = b_in.shape[1]
    N = nh * NS
    OC = D // NH // NS
    RB = 4
    nchunk = HP // CHUNK
    tok_own = T // NH
    dims = (T, H, HP, HD, NS, NH, NCTX, LV, OC, RB)
    V = pltpu.VMEM
    scratch = [
        V((T, D), BF16), V((D, HP), BF16), V((NH, OC, inner), BF16), V((T, HP), BF16),
        V((nh, T), BF16), V((nh, T), BF16), V((T, N), BF16), V((T, N), BF16), V((N, T), BF16), V((N, T), BF16),
        V((LV + 3, T, 2 * H), BF16), V((nchunk, T, CHUNK // HD), F32), V((nchunk, 8, T), F32), V((nchunk, 8, T), F32),
        V((LV, 8, HP), F32), V((LV, 8, HP), F32), V((LV, 8, HP), F32),
        V((LV, T, HP), BF16), V((T, HP), BF16), V((T, HP), BF16), V((LV, N, HP), F32), V((N, HP), F32),
        V((LV, N, HP), BF16), V((LV, N, HP), BF16), V((LV, N, HP), BF16), V((LV, N, HP), BF16), V((N, HP), F32),
        V((T, T), F32), V((T, T), BF16), V((T, T), F32), V((T, HP), F32), V((NS, T, HP), BF16),
        V((NH - 1, T, OC), BF16), V((NH - 1, T, OC), BF16), V((T, OC), F32),
        V((NS, 2, T, nh), BF16), V((NH * NS - 1, 2, tok_own, nh), BF16),
    ]
    S = pltpu.SemaphoreType.DMA
    scratch += [S((3 + NH,)), S((2, 2)), S((2, LV)), S((2, LV)), S((2, LV)), S((2, RB)),
                S((2, (NH - 1) * RB)), S((2, NH * NS - 1))]
    vm = pl.BlockSpec(memory_space=pltpu.VMEM)
    hb = pl.BlockSpec(memory_space=pl.ANY)
    grad_inputs, grad_b, grad_c = pl.pallas_call(
        functools.partial(kernel, dims),
        out_shape=(jax.ShapeDtypeStruct((T, OC), BF16), jax.ShapeDtypeStruct((nh, tok_own), BF16),
                   jax.ShapeDtypeStruct((nh, tok_own), BF16)),
        in_specs=[hb, hb, hb, vm, vm, vm, vm],
        out_specs=(vm, vm, vm),
        scratch_shapes=scratch,
        compiler_params=pltpu.CompilerParams(
            collective_id=0, has_side_effects=True, vmem_limit_bytes=56 * 2 ** 20),
    )(inputs, w_in, out_grad, b_in.T, c_in.T, log_decay, level_weight)
    outs = (grad_inputs, grad_b, grad_c)
    grad_inputs, grad_b, grad_c = pl.pallas_call(
        hand_out, out_shape=tuple(jax.ShapeDtypeStruct(o.shape, o.dtype) for o in outs),
        in_specs=[vm] * 3, out_specs=(vm,) * 3)(*outs)
    return grad_inputs, grad_b.T, grad_c.T


def solution(mesh):
    in_specs = (
        P(("groups", "ctx"), None),
        P(None, "head"),
        P(("groups", "ctx"), "sub"),
        P(("groups", "ctx"), "sub"),
        P("head", ("groups", "ctx")),
        P(None, "head", ("groups", "ctx")),
        P(("groups", "ctx"), "head"),
    )
    out_specs = (
        P(("groups", "ctx"), ("head", "sub")),
        P(("groups", "ctx", "head"), "sub"),
        P(("groups", "ctx", "head"), "sub"),
    )
    return jax.shard_map(shards, mesh=mesh, in_specs=in_specs, out_specs=out_specs, check_vma=False)
```
